256 devices in a mesh: micro: 8 (over x, y_hi), macro: 32 (over z, y_lo, core).
Axes of the slice: x: 4, y: 4 (y_hi: 2, y_lo: 2; y = y_hi * 2 + y_lo), z: 8, core: 2. Of those that a mesh axis runs over, the one named last changes fastest.
Arguments:
- interaction: bfloat16 [32, 6, 1024, 6, 1024], P('macro', None, 'micro'), may hold values from -0.013671875 to 0.013671875
- cluster_moduli: float32 [32, 3, 1024], P('macro', None, 'micro'), may hold values from 0.5 to 2
- cluster_fraction: float32 [32, 1024], P('macro', 'micro'), may hold values from 0.1 to 10
- plastic_flag: int32 [32, 1024], P('macro', 'micro'), may hold values 0 or 1
- micro_id: int32 [2048, 1], P('macro'), may hold values from 0 to 31; in each aligned block of 64 rows (0 to 63, 64 to 127, ...) at most 6 rows name the same one
- macro_strain: float32 [2048, 6], P('macro'), may hold values from -6 to 6
- cluster_state: float32 [2048, 6, 1024], P('macro', None, 'micro'), may hold values from -4 to 4
Outputs:
- cluster_strain: float32 [2048, 6, 1024], P('macro', None, 'micro')
- hom_stress: float32 [6, 2048], P(None, 'macro')
- residual: float32 [3, 2048], P(None, 'macro')
The draws below stay inside these ranges and needn't reach their ends.
Inputs may be any that keep to these rules, and one draw needn't show every extreme that they name: `micro_id`: in each aligned block of 64 points (one slab), no microstructure is named more than 6 times, and in some block one is named exactly 6 times.
All inputs are finite; a program needn't handle non-finite values. No bound on the sum of `plastic_flag` on one device may be relied on, other than what follows from the above.
Results may differ from the reference program's by a relative error of at most 0.00074.
Values may be sent and summed in bfloat16 or wider, within the bound.
A program may use at most 64 MiB of HBM per device.

```python
import math
import jax
import jax.numpy as jnp
import numpy as np
from jax import lax

K = 1024
ITERS = 3
GX = 8
GY = 8
PT_DEV = 64
MICROS = 32
CAP = 6
NPTS = 2048
NZ = 32
N_MACRO = 32


def place_ends(values, key, smallest, largest):
    place = [jax.random.randint(jax.random.fold_in(key, axis), (), 0, length) for axis, length in enumerate(values.shape)]
    longest = values.shape.index(max(values.shape))
    next_to = place[:longest] + [(place[longest] + 1) % values.shape[longest]] + place[longest + 1:]
    return values.at[tuple(place)].set(smallest).at[tuple(next_to)].set(largest)


def shard_levels(key, shape, cuts, smallest, largest):
    gain, own = 1.0, jax.random.fold_in(key, 6)
    for position, shards_of in cuts:
        draws = jnp.exp(jax.random.uniform(jax.random.fold_in(own, position), (shards_of,), jnp.float32, smallest / len(cuts), largest / len(cuts)))
        gain = gain * jnp.repeat(draws, shape[position] // shards_of).reshape([-1 if axis == position else 1 for axis in range(len(shape))])
    return gain


def shared_out(rng, own, number, rows, count, top, bound, lean):
    ranking = jax.random.permutation(rng, count)
    crowded, ordinary = shares(count, rows * top, bound, lean, True), shares(count, rows * top, bound, lean, False)
    places = jnp.arange(count)

    def named(sizes, turn):
        used = int((sizes > 0).sum())
        fixed = max(1, used // 4)
        passed = fixed + (places - fixed + turn * (used - fixed)) % max(1, count - fixed)
        return jnp.zeros((count,), jnp.int32).at[ranking[jnp.where(places < fixed, places, passed)]].set(jnp.asarray(sizes, jnp.int32))

    sizes = jnp.where(number % 4 == 0, named(crowded, number // 4), named(ordinary, number - number // 4 - 1))
    mixed = jax.random.permutation(jax.random.fold_in(own, 3), count)
    giver, taker = mixed[0:count // 2 * 2:2], mixed[1:count // 2 * 2:2]
    margin = jnp.minimum(sizes[giver] - 1, bound - sizes[taker]) // 2
    margin = jnp.where((giver == ranking[0]) | (taker == ranking[0]) | (sizes[taker] == 0), 0, jnp.maximum(margin, 0))
    passed = jax.random.randint(jax.random.fold_in(own, 4), (count // 2,), 0, 1 << 20) % (margin + 1)
    sizes = sizes.at[giver].add(-passed).at[taker].add(passed)
    members = jnp.searchsorted(jnp.cumsum(sizes), jnp.arange(rows * top), side="right").astype(jnp.int32)
    listing = members.reshape(top, rows).T
    listing = listing[jax.random.permutation(jax.random.fold_in(own, 1), rows)]
    turn = jax.random.randint(jax.random.fold_in(own, 2), (rows, 1), 0, top)
    return jnp.take_along_axis(listing, (jnp.arange(top)[None, :] + turn) % top, axis=1)


def shares(number_of, total, reach, slope, full):
    portions = [(1 << 20) // math.isqrt(grade ** slope) + 1 for grade in range(1, number_of + 1)]
    largest = reach if full else min(reach, max(-(-total // number_of), total * portions[0] // sum(portions)))
    least = 1 if total - largest >= number_of - 1 else 0
    given, spare = [largest] + [least] * (number_of - 1), total - largest - least * (number_of - 1)
    while spare > 0:
        movable = [i for i in range(1, number_of) if given[i] < largest] or [i for i in range(1, number_of) if given[i] < reach]
        pool, budget = sum([portions[i] for i in movable]), spare
        for i in movable:
            more = min(reach - given[i], max(1, budget * portions[i] // pool), spare)
            given[i] = given[i] + more
            spare = spare - more
    return np.array(given)


def centred(rng, shape, width, limit, split=(), kind=jnp.bfloat16):
    entries = jax.random.normal(rng, shape, jnp.float32) * width
    if len(split) > 0:
        entries = shard_levels(rng, shape, split, -0.22, 0.18) * entries
    return jnp.clip(entries, min=-limit, max=limit).astype(kind)


def setup_inputs(seed: int = 0) -> dict:
    arg_keys = jax.random.split(jax.random.key(seed), 8)
    interaction = centred(arg_keys[0], (MICROS, 6, K, 6, K), (192 * K) ** -0.5, 0.013671875, ((0, 32), (2, 8)))
    cluster_moduli = jnp.clip(jnp.exp(math.log(2.0) - 1.3862944 * jax.random.uniform(arg_keys[1], (MICROS, 3, K), jnp.float32) ** shard_levels(arg_keys[1], (MICROS, 3, K), ((0, 32), (2, 8)), -0.2, 0.2)), 0.5, 2.0)
    cluster_fraction = jnp.clip(jnp.exp(math.log(10.0) - 4.6051702 * jax.random.uniform(arg_keys[2], (MICROS, K), jnp.float32) ** shard_levels(arg_keys[2], (MICROS, K), ((0, 32), (1, 8)), -0.2, 0.2)), 0.1, 10.0)
    plastic_flag = place_ends((jax.random.randint(arg_keys[3], (MICROS, K), 0, 2) < 1).astype(jnp.int32), jax.random.fold_in(arg_keys[3], 1), 0, 1)
    micro_id_keys = jax.random.split(jax.random.fold_in(arg_keys[4], 1), NPTS // PT_DEV)
    micro_id_turns = jax.random.permutation(jax.random.fold_in(arg_keys[4], 3), NPTS // PT_DEV)
    micro_id = jax.vmap(lambda own, number: shared_out(jax.random.fold_in(arg_keys[4], 2), own, number, PT_DEV, MICROS, 1, CAP, 2))(micro_id_keys, micro_id_turns).reshape((NPTS, 1))
    macro_strain = centred(arg_keys[5], (NPTS, 6), 1.0, 6.0, ((0, 32),), jnp.float32)
    cluster_state = centred(arg_keys[6], (NPTS, 6, K), 0.5, 4.0, ((0, 32), (2, 8)), jnp.float32)
    return {"interaction": interaction, "cluster_moduli": cluster_moduli, "cluster_fraction": cluster_fraction, "plastic_flag": plastic_flag, "micro_id": micro_id, "macro_strain": macro_strain, "cluster_state": cluster_state}


LAM_REF = 1.0
MU_REF = 1.0

def stress_update(strain, moduli, plastic):
    lame_first = moduli[0]
    shear_mod = moduli[1]
    yield_level = moduli[2]
    volume_part = strain[:, 0] + strain[:, 1] + strain[:, 2]
    normal_dev = strain[:, 0:3] - volume_part[:, None] / 3.0
    shear_part = strain[:, 3:6]
    dev_square = lax.optimization_barrier(jnp.sum(normal_dev * normal_dev, axis=1)) + 2.0 * lax.optimization_barrier(jnp.sum(shear_part * shear_part, axis=1))
    softening = 1.0 / jnp.sqrt(1.0 + 4.0 * shear_mod * shear_mod * dev_square / (yield_level * yield_level))
    factor = 1.0 + plastic.astype(jnp.float32) * (softening - 1.0)
    bulk_stress = (lame_first + 2.0 * shear_mod / 3.0) * volume_part
    deviator = jnp.concatenate([normal_dev, shear_part], axis=1)
    scaled = 2.0 * (shear_mod * factor)[:, None] * deviator
    stress = jnp.concatenate([scaled[:, 0:3] + bulk_stress[:, None], scaled[:, 3:6]], axis=1)
    ref_normal = LAM_REF * volume_part[:, None] + 2.0 * MU_REF * strain[:, 0:3]
    ref_shear = 2.0 * MU_REF * strain[:, 3:6]
    reference_stress = jnp.concatenate([ref_normal, ref_shear], axis=1)
    return (stress, stress - reference_stress)

def central_diff(field, axis_number):
    widths = [(1, 1) if dim_number == axis_number else (0, 0) for dim_number in range(field.ndim)]
    padded = jnp.pad(field, widths)
    length = field.shape[axis_number]
    upper = lax.slice_in_dim(padded, 2, length + 2, axis=axis_number)
    lower = lax.slice_in_dim(padded, 0, length, axis=axis_number)
    return 0.5 * (upper - lower)

def reference(interaction, cluster_moduli, cluster_fraction, plastic_flag, micro_id, macro_strain, cluster_state):
    slots_per = N_MACRO * CAP
    owner_id = micro_id[:, 0]
    blocks = owner_id.reshape(N_MACRO, PT_DEV)
    onehot = (blocks[:, :, None] == jnp.arange(MICROS, dtype=jnp.int32)[None, None, :]).astype(jnp.int32)
    before = jnp.cumsum(onehot, axis=1) - onehot
    rank_slot = lax.optimization_barrier(jnp.sum(before * onehot, axis=2)).reshape(NPTS)
    source = jnp.arange(NPTS, dtype=jnp.int32) // PT_DEV
    slot_index = source * CAP + rank_slot
    flat_index = (owner_id * slots_per + slot_index).astype(jnp.int32)
    table = jnp.full((MICROS * slots_per,), NPTS, jnp.int32).at[flat_index].set(jnp.arange(NPTS, dtype=jnp.int32))
    table = table.reshape(MICROS, slots_per)
    state_pad = jnp.concatenate([cluster_state, jnp.zeros((1, 6, K), jnp.float32)], axis=0)
    strain_pad = jnp.concatenate([macro_strain, jnp.zeros((1, 6), jnp.float32)], axis=0)

    def solve_group(micro_index):
        row_index = table[micro_index]
        strain = state_pad[row_index]
        target = strain_pad[row_index]
        coupling = lax.dynamic_index_in_dim(interaction, micro_index, 0, keepdims=False).reshape(6 * K, 6 * K)
        moduli = lax.dynamic_index_in_dim(cluster_moduli, micro_index, 0, keepdims=False)
        plastic = lax.dynamic_index_in_dim(plastic_flag, micro_index, 0, keepdims=False)
        fraction = lax.dynamic_index_in_dim(cluster_fraction, micro_index, 0, keepdims=False)
        for iteration in range(ITERS):
            stress, polarization = stress_update(strain, moduli, plastic)
            polar_low = polarization.astype(jnp.bfloat16).reshape(slots_per, 6 * K)
            coupled = lax.dot_general(polar_low, coupling, (((1,), (1,)), ((), ())), preferred_element_type=jnp.float32)
            strain = target[:, :, None] - coupled.reshape(slots_per, 6, K)
        stress, polarization = stress_update(strain, moduli, plastic)
        averaged = lax.optimization_barrier(jnp.sum(stress * fraction[None, None, :], axis=2)) / jnp.sum(fraction)
        return (strain, averaged)
    strains, averages = lax.map(solve_group, jnp.arange(MICROS, dtype=jnp.int32))
    cluster_strain = strains.reshape(MICROS * slots_per, 6, K)[flat_index]
    point_stress = averages.reshape(MICROS * slots_per, 6)[flat_index]
    hom_stress = point_stress.T
    grid = hom_stress.reshape(6, NZ, GX, GY)
    along_x = central_diff(grid, 2)
    along_y = central_diff(grid, 3)
    along_z = central_diff(grid, 1)
    res_x = along_x[0] + along_y[5] + along_z[4]
    res_y = along_x[5] + along_y[1] + along_z[3]
    res_z = along_x[4] + along_y[3] + along_z[2]
    residual = jnp.stack([res_x, res_y, res_z], axis=0).reshape(3, NPTS)
    return (cluster_strain, hom_stress, residual)
```

```python
import functools

import jax
import jax.numpy as jnp
from jax import lax
from jax.experimental import pallas as pl
from jax.experimental.pallas import tpu as pltpu
from jax.sharding import PartitionSpec as P

MESH = pl.DeviceIdType.MESH
HIGHEST = lax.Precision.HIGHEST
ITERS = 3
CHUNKS = 3
HOMES = 32
ROWS = 64
STAGES = ITERS * CHUNKS
MSG = 16


def law(strain, lam, mu, hard, flag):
    tr = strain[0] + strain[1] + strain[2]
    third = tr / 3.0
    dev = [strain[0] - third, strain[1] - third, strain[2] - third, strain[3], strain[4], strain[5]]
    square = (dev[0] * dev[0] + dev[1] * dev[1] + dev[2] * dev[2]) + 2.0 * (
        dev[3] * dev[3] + dev[4] * dev[4] + dev[5] * dev[5]
    )
    soft = lax.rsqrt(1.0 + hard * square)
    scale = 2.0 * (mu * (1.0 + flag * (soft - 1.0)))
    bulk = (lam + 2.0 * mu / 3.0) * tr
    return [scale * dev[a] + bulk if a < 3 else scale * dev[a] for a in range(6)], tr


def kernel(
    w_hbm, moduli_ref, fraction_ref, plastic_ref, id_ref, strain_ref, state_ref,
    home_ref, hom_ref, res_ref,
    w, g, tx, rx, ty, ry, tg, ebuf, pacc, px, rt, rr, st, sn,
    w_sem, in_send, in_recv, ag_send, ag_recv, out_send, out_recv, p_send, p_recv, r_send, r_recv, s_send, s_recv,
):
    micro, me = lax.axis_index("micro"), lax.axis_index("macro")
    x, r = micro // 2, micro % 2
    xl, xr, xo = lax.rem(x + 3, 4), lax.rem(x + 1, 4), lax.rem(x + 2, 4)
    left, right, across = xl * 2 + r, xr * 2 + r, x * 2 + (1 - r)
    across_left, across_right = xl * 2 + (1 - r), xr * 2 + (1 - r)

    load_w = pltpu.make_async_copy(w_hbm, w, w_sem)
    load_w.start()

    barrier = pltpu.get_barrier_semaphore()

    def greet_macro(d, carry):
        pl.semaphore_signal(barrier, inc=1, device_id=(micro, lax.rem(me + d, HOMES)), device_id_type=MESH)
        return carry

    def greet_micro(d, carry):
        pl.semaphore_signal(barrier, inc=1, device_id=(lax.rem(micro + d, 8), me), device_id_type=MESH)
        return carry

    lax.fori_loop(1, HOMES, greet_macro, 0)
    lax.fori_loop(1, 8, greet_micro, 0)

    ids = id_ref[...]
    down = lax.broadcasted_iota(jnp.int32, (64, 64), 0)
    along = lax.broadcasted_iota(jnp.int32, (64, 64), 1)
    id_row = jnp.broadcast_to(ids, (64, 64))
    id_col = jnp.broadcast_to(jnp.sum(jnp.where(down == along, id_row, 0), axis=1, keepdims=True), (64, 64))
    same = id_row == id_col
    slot_row = jnp.sum(jnp.where(same & (down < along), 1, 0), axis=0, keepdims=True) * HOMES + ids
    slot_col = jnp.sum(jnp.where(same & (along < down), 1, 0), axis=1, keepdims=True) * HOMES + jnp.sum(
        jnp.where(down == along, id_row, 0), axis=1, keepdims=True
    )
    slot_col = jnp.broadcast_to(slot_col, (64, 64))
    slot_row = jnp.broadcast_to(slot_row, (64, 64))
    st[...] = jnp.concatenate([slot_row[0:8], jnp.full((8, 64), -1, jnp.int32)], axis=1)

    strain_cols = jnp.concatenate([strain_ref[...], jnp.zeros((122, 64), jnp.float32)], axis=0)
    for c in range(CHUNKS):
        pick = jnp.where(down + c * 64 == slot_row, 1.0, 0.0)
        for b in range(6):
            rows = jnp.dot(pick, state_ref[b], precision=HIGHEST, preferred_element_type=jnp.float32)
            for q in range(2):
                tx[c, pl.ds(b * 2 + q, HOMES, stride=MSG), :] = rows[q * 32 : (q + 1) * 32]
        rows = lax.dot_general(
            pick, strain_cols, (((1,), (1,)), ((), ())), precision=HIGHEST, preferred_element_type=jnp.float32
        )
        for q in range(2):
            tx[c, pl.ds(12 + q, HOMES, stride=MSG), :] = rows[q * 32 : (q + 1) * 32]
            tx[c, pl.ds(14 + q, HOMES, stride=MSG), :] = jnp.zeros((HOMES, 128), jnp.float32)
            ty[c, pl.ds(12 + q, HOMES, stride=MSG), :] = jnp.zeros((HOMES, 128), jnp.float32)
            ty[c, pl.ds(14 + q, HOMES, stride=MSG), :] = jnp.zeros((HOMES, 128), jnp.float32)
    pacc[...] = jnp.zeros((128, 128), jnp.float32)

    pl.semaphore_wait(barrier, 31 + 7)

    def exchange(src, dst, c, send_sem, recv_sem):
        def body(d, carry):
            to = lax.rem(me + d, HOMES)
            pltpu.make_async_remote_copy(
                src_ref=src.at[c, pl.ds(pl.multiple_of(to * MSG, MSG), MSG), :],
                dst_ref=dst.at[c, pl.ds(pl.multiple_of(me * MSG, MSG), MSG), :],
                send_sem=send_sem.at[c],
                recv_sem=recv_sem.at[c],
                device_id=(micro, to),
                device_id_type=MESH,
            ).start()
            return carry

        lax.fori_loop(1, HOMES, body, 0)
        own = pl.ds(pl.multiple_of(me * MSG, MSG), MSG)
        dst[c, own, :] = src[c, own, :]

    def drain(ref, sem):
        pltpu.make_async_copy(ref, ref, sem).wait()

    for c in range(CHUNKS):
        exchange(tx, rx, c, in_send, in_recv)
    for side in range(2):
        pltpu.make_async_remote_copy(
            src_ref=st,
            dst_ref=sn.at[1 - side],
            send_sem=s_send.at[side],
            recv_sem=s_recv.at[1 - side],
            device_id=(micro, lax.rem(me + HOMES - 1 + 2 * side, HOMES)),
            device_id_type=MESH,
        ).start()

    lam, mu, level = moduli_ref[0], moduli_ref[1], moduli_ref[2]
    hard = 4.0 * mu * mu / (level * level)
    flag = plastic_ref[...].astype(jnp.float32)
    fraction = fraction_ref[...]
    total = jnp.sum(fraction, axis=1, keepdims=True)

    def send(s, block, low, high, to, kind):
        pltpu.make_async_remote_copy(
            src_ref=g.at[s, block, low:high],
            dst_ref=g.at[s, block, low:high],
            send_sem=ag_send.at[s],
            recv_sem=ag_recv.at[s, kind],
            device_id=(to, me),
            device_id_type=MESH,
        ).start()

    def polarize(s, strain):
        stress, tr = law(strain, lam, mu, hard, flag)
        for a in range(6):
            tau = stress[a] - (tr + 2.0 * strain[a]) if a < 3 else stress[a] - 2.0 * strain[a]
            g[s, micro, a] = tau.astype(jnp.bfloat16)

    def period(p, carry):
        @pl.when(p < CHUNKS)
        def _():
            drain(rx.at[p, 0 : 31 * MSG], in_recv.at[p])
            strain = [
                jnp.concatenate([rx[p, pl.ds(b * 2 + q, HOMES, stride=MSG), :] for q in range(2)], axis=0)
                for b in range(6)
            ]
            tg[p] = jnp.concatenate([rx[p, pl.ds(12 + q, HOMES, stride=MSG), :] for q in range(2)], axis=0)
            polarize(p, strain)

        @pl.when(p < STAGES)
        def _():
            send(p, micro, 0, 6, right, 0)
            send(p, micro, 0, 6, left, 1)
            send(p, micro, 0, 6, across, 2)

        @pl.when((p >= 1) & (p < STAGES + 1))
        def _():
            s = p - 1
            drain(g.at[s, 0], ag_recv.at[s, 0])
            send(s, left, 0, 3, right, 5)
            send(s, left, 0, 3, across, 3)
            drain(g.at[s, 0], ag_recv.at[s, 1])
            send(s, right, 3, 6, left, 5)
            send(s, right, 3, 6, across, 4)
            drain(g.at[s, 0], ag_recv.at[s, 2])
            send(s, across, 0, 3, left, 5)
            send(s, across, 3, 6, right, 5)

        @pl.when(p >= 2)
        def _():
            s = p - 2
            c = lax.rem(s, CHUNKS)
            drain(g.at[s, 0, 0:3], ag_recv.at[s, 3])
            send(s, across_left, 0, 3, right, 5)
            drain(g.at[s, 0, 0:3], ag_recv.at[s, 4])
            send(s, across_right, 3, 6, left, 5)
            @pl.when(p == 2)
            def _():
                load_w.wait()

            drain(g.at[s, 0:3], ag_recv.at[s, 5])
            columns = [jnp.concatenate([g[s, j, b] for b in range(6)], axis=1) for j in range(8)]
            target = tg[c]
            for a in range(6):
                acc = jnp.zeros((128, ROWS), jnp.float32)
                for j in range(8):
                    rows = jnp.concatenate([w[a, b, :, j * 128 : (j + 1) * 128] for b in range(6)], axis=1)
                    acc = acc + lax.dot_general(
                        rows, columns[j], (((1,), (1,)), ((), ())), preferred_element_type=jnp.float32
                    )
                ebuf[a] = target[:, a : a + 1] - acc.T
            strain = [ebuf[a] for a in range(6)]

            @pl.when(s < STAGES - CHUNKS)
            def _():
                polarize(s + CHUNKS, strain)

            @pl.when(s >= STAGES - CHUNKS)
            def _():
                for b in range(6):
                    for q in range(2):
                        ty[c, pl.ds(b * 2 + q, HOMES, stride=MSG), :] = ebuf[b, q * 32 : (q + 1) * 32]
                exchange(ty, ry, c, out_send, out_recv)
                stress, _ = law(strain, lam, mu, hard, flag)
                lane = lax.broadcasted_iota(jnp.int32, (ROWS, 128), 1)
                sums = pacc[0:ROWS]
                for a in range(6):
                    part = jnp.sum(stress[a] * fraction, axis=1, keepdims=True)
                    sums = jnp.where(lane == c * 8 + a, part, sums)
                pacc[0:ROWS] = sums

        return carry

    lax.fori_loop(0, STAGES + 2, period, 0)

    sums = pacc[...].T[0 : 8 * CHUNKS]
    row = lax.broadcasted_iota(jnp.int32, (8 * CHUNKS, 128), 0)
    px[micro] = jnp.where(row == 6, total, sums)

    def share(d, carry):
        pltpu.make_async_remote_copy(
            src_ref=px.at[micro],
            dst_ref=px.at[micro],
            send_sem=p_send,
            recv_sem=p_recv,
            device_id=(lax.rem(micro + d, 8), me),
            device_id_type=MESH,
        ).start()
        return carry

    lax.fori_loop(1, 8, share, 0)
    drain(px.at[0:7], p_recv)
    sums = px[0]
    for i in range(1, 8):
        sums = sums + px[i]
    mean = sums / sums[6:7]
    mean = jnp.concatenate([mean, jnp.zeros((128 - 8 * CHUNKS, 128), jnp.float32)], axis=0).T
    for d in range(3):
        for q in range(2):
            part = mean[q * 32 : (q + 1) * 32]
            if d != 1:
                part = pltpu.roll(part, 1 if d == 0 else 31, 0)
            rt[pl.ds(d * 2 + q, HOMES, stride=8), :] = part
    for spare in (6, 7):
        rt[pl.ds(spare, HOMES, stride=8), :] = jnp.zeros((HOMES, 128), jnp.float32)

    def give(d, carry):
        to = lax.rem(me + d, HOMES)
        pltpu.make_async_remote_copy(
            src_ref=rt.at[pl.ds(pl.multiple_of(to * 8, 8), 8), :],
            dst_ref=rr.at[pl.ds(pl.multiple_of(me * 8, 8), 8), :],
            send_sem=r_send,
            recv_sem=r_recv,
            device_id=(micro, to),
            device_id_type=MESH,
        ).start()
        return carry

    lax.fori_loop(1, HOMES, give, 0)
    own = pl.ds(pl.multiple_of(me * 8, 8), 8)
    rr[own, :] = rt[own, :]

    for c in range(CHUNKS):
        drain(ry.at[c, 0 : 31 * MSG], out_recv.at[c])
        pick = jnp.where(along + c * 64 == slot_col, 1.0, 0.0)
        for b in range(6):
            rows = jnp.concatenate([ry[c, pl.ds(b * 2 + q, HOMES, stride=MSG), :] for q in range(2)], axis=0)
            part = jnp.dot(pick, rows, precision=HIGHEST, preferred_element_type=jnp.float32)
            home_ref[b] = part if c == 0 else home_ref[b] + part

    for side in range(2):
        drain(sn.at[side], s_recv.at[side])
    drain(rr.at[0 : 31 * 8], r_recv)
    slots = [sn[0][0:1], st[0:1], sn[1][0:1]]
    down2 = lax.broadcasted_iota(jnp.int32, (64, 128), 0)
    hom = []
    for d in range(3):
        rows = jnp.concatenate([rr[pl.ds(d * 2 + q, HOMES, stride=8), :] for q in range(2)], axis=0).T
        slab = jnp.zeros((8, 128), jnp.float32)
        for c in range(CHUNKS):
            pick = jnp.where(down2 + c * 64 == jnp.broadcast_to(slots[d], (64, 128)), 1.0, 0.0)
            slab = slab + jnp.dot(
                rows[c * 8 : (c + 1) * 8], pick, precision=HIGHEST, preferred_element_type=jnp.float32
            )
        hom.append(slab)
    here = hom[1]
    hom_ref[...] = here[0:6, 0:64]
    lane = lax.broadcasted_iota(jnp.int32, (8, 128), 1)
    along_x = 0.5 * (pltpu.roll(here, 120, 1) - pltpu.roll(here, 8, 1))
    above = jnp.where(lane % 8 == 7, 0.0, pltpu.roll(here, 127, 1))
    below = jnp.where(lane % 8 == 0, 0.0, pltpu.roll(here, 1, 1))
    along_y = 0.5 * (above - below)
    along_z = 0.5 * (jnp.where(me == HOMES - 1, 0.0, hom[2]) - jnp.where(me == 0, 0.0, hom[0]))
    res_x = along_x[0:1] + along_y[5:6] + along_z[4:5]
    res_y = along_x[5:6] + along_y[1:2] + along_z[3:4]
    res_z = along_x[4:5] + along_y[3:4] + along_z[2:3]
    res_ref[...] = jnp.concatenate([res_x, res_y, res_z], axis=0)[:, 0:64]

    for c in range(CHUNKS):
        drain(tx.at[c, 0 : 31 * MSG], in_send.at[c])
        drain(ty.at[c, 0 : 31 * MSG], out_send.at[c])
    for side in range(2):
        drain(st, s_send.at[side])

    def sent(s, carry):
        drain(g.at[s, 0:7], ag_send.at[s])
        return carry

    lax.fori_loop(0, STAGES, sent, 0)
    drain(px.at[0:7], p_send)
    drain(rt.at[0 : 31 * 8], r_send)


def local(interaction, cluster_moduli, cluster_fraction, plastic_flag, micro_id, macro_strain, cluster_state):
    vmem = pl.BlockSpec(memory_space=pltpu.VMEM)
    home, hom, res = pl.pallas_call(
        kernel,
        out_shape=(
            jax.ShapeDtypeStruct((6, 64, 128), jnp.float32),
            jax.ShapeDtypeStruct((6, 64), jnp.float32),
            jax.ShapeDtypeStruct((3, 64), jnp.float32),
        ),
        in_specs=[pl.BlockSpec(memory_space=pl.ANY)] + [vmem] * 6,
        out_specs=(vmem, vmem, vmem),
        scratch_shapes=[
            pltpu.VMEM((6, 6, 128, 1024), jnp.bfloat16),
            pltpu.VMEM((STAGES, 8, 6, ROWS, 128), jnp.bfloat16),
            pltpu.VMEM((CHUNKS, HOMES * MSG, 128), jnp.float32),
            pltpu.VMEM((CHUNKS, HOMES * MSG, 128), jnp.float32),
            pltpu.VMEM((CHUNKS, HOMES * MSG, 128), jnp.float32),
            pltpu.VMEM((CHUNKS, HOMES * MSG, 128), jnp.float32),
            pltpu.VMEM((CHUNKS, ROWS, 128), jnp.float32),
            pltpu.VMEM((6, ROWS, 128), jnp.float32),
            pltpu.VMEM((128, 128), jnp.float32),
            pltpu.VMEM((8, 8 * CHUNKS, 128), jnp.float32),
            pltpu.VMEM((HOMES * 8, 128), jnp.float32),
            pltpu.VMEM((HOMES * 8, 128), jnp.float32),
            pltpu.VMEM((8, 128), jnp.int32),
            pltpu.VMEM((2, 8, 128), jnp.int32),
            pltpu.SemaphoreType.DMA,
            pltpu.SemaphoreType.DMA((CHUNKS,)),
            pltpu.SemaphoreType.DMA((CHUNKS,)),
            pltpu.SemaphoreType.DMA((STAGES,)),
            pltpu.SemaphoreType.DMA((STAGES, 6)),
            pltpu.SemaphoreType.DMA((CHUNKS,)),
            pltpu.SemaphoreType.DMA((CHUNKS,)),
            pltpu.SemaphoreType.DMA,
            pltpu.SemaphoreType.DMA,
            pltpu.SemaphoreType.DMA,
            pltpu.SemaphoreType.DMA,
            pltpu.SemaphoreType.DMA((2,)),
            pltpu.SemaphoreType.DMA((2,)),
        ],
        compiler_params=pltpu.CompilerParams(
            collective_id=0, has_side_effects=True, vmem_limit_bytes=48 * 2**20
        ),
    )(
        jnp.transpose(interaction[0], (0, 2, 1, 3)),
        jnp.transpose(cluster_moduli, (1, 0, 2)),
        cluster_fraction,
        plastic_flag,
        micro_id.reshape(1, -1),
        macro_strain.T,
        jnp.transpose(cluster_state, (1, 0, 2)),
    )
    return jnp.transpose(home, (1, 0, 2)), hom, res


def solution(mesh):
    placed = (
        P("macro", None, "micro", None, None),
        P("macro", None, "micro"),
        P("macro", "micro"),
        P("macro", "micro"),
        P("macro", None),
        P("macro", None),
        P("macro", None, "micro"),
    )
    return jax.shard_map(
        local,
        mesh=mesh,
        in_specs=placed,
        out_specs=(P("macro", None, "micro"), P(None, "macro"), P(None, "macro")),
        check_vma=False,
    )
```

```python
import functools

import jax
import jax.numpy as jnp
from jax import lax
from jax.experimental import pallas as pl
from jax.experimental.pallas import tpu as pltpu
from jax.sharding import PartitionSpec as P

MESH = pl.DeviceIdType.MESH
HIGHEST = lax.Precision.HIGHEST
ITERS = 3
CHUNKS = 3
HOMES = 32
ROWS = 64
STAGES = ITERS * CHUNKS
MSG = 16


def law(strain, lam, mu, hard, flag):
    tr = strain[0] + strain[1] + strain[2]
    third = tr / 3.0
    dev = [strain[0] - third, strain[1] - third, strain[2] - third, strain[3], strain[4], strain[5]]
    square = (dev[0] * dev[0] + dev[1] * dev[1] + dev[2] * dev[2]) + 2.0 * (
        dev[3] * dev[3] + dev[4] * dev[4] + dev[5] * dev[5]
    )
    soft = lax.rsqrt(1.0 + hard * square)
    scale = 2.0 * (mu * (1.0 + flag * (soft - 1.0)))
    bulk = (lam + 2.0 * mu / 3.0) * tr
    return [scale * dev[a] + bulk if a < 3 else scale * dev[a] for a in range(6)], tr


def kernel(
    w_hbm, moduli_hbm, fraction_hbm, plastic_hbm, id_hbm, strain_hbm, state_hbm,
    home_ref, hom_ref, res_ref,
    w, moduli_ref, fraction_ref, plastic_ref, id_ref, strain_ref, state_ref, acc, g, tx, rx, ty, ry, tg, ebuf, pacc, px, rt, rr, st, sn,
    w_sem, i_sem, in_send, in_recv, ag_send, ag_recv, out_send, out_recv, p_send, p_recv, r_send, r_recv, s_send, s_recv,
):
    micro, me = lax.axis_index("micro"), lax.axis_index("macro")
    x, r = micro // 2, micro % 2
    xl, xr, xo = lax.rem(x + 3, 4), lax.rem(x + 1, 4), lax.rem(x + 2, 4)
    left, right, across = xl * 2 + r, xr * 2 + r, x * 2 + (1 - r)
    across_left, across_right = xl * 2 + (1 - r), xr * 2 + (1 - r)

    loads = [
        pltpu.make_async_copy(src, dst, i_sem.at[i])
        for i, (src, dst) in enumerate(
            [
                (id_hbm, id_ref), (state_hbm, state_ref), (strain_hbm, strain_ref),
                (moduli_hbm, moduli_ref), (fraction_hbm, fraction_ref), (plastic_hbm, plastic_ref),
            ]
        )
    ]
    for load in loads:
        load.start()
    load_w = pltpu.make_async_copy(w_hbm, w, w_sem)
    load_w.start()

    barrier = pltpu.get_barrier_semaphore()

    def far(i):
        half = (i + 1) // 2
        return lax.rem(me + HOMES + 16 + half * (1 - 2 * (i % 2)), HOMES)

    def greet_macro(i, carry):
        pl.semaphore_signal(barrier, inc=1, device_id=(micro, far(i)), device_id_type=MESH)
        return carry

    def greet_micro(d, carry):
        pl.semaphore_signal(barrier, inc=1, device_id=(lax.rem(micro + d, 8), me), device_id_type=MESH)
        return carry

    lax.fori_loop(0, HOMES - 1, greet_macro, 0)
    lax.fori_loop(1, 8, greet_micro, 0)

    for load in loads:
        load.wait()
    ids = id_ref[...]
    down = lax.broadcasted_iota(jnp.int32, (64, 64), 0)
    along = lax.broadcasted_iota(jnp.int32, (64, 64), 1)
    id_row = jnp.broadcast_to(ids, (64, 64))
    id_col = jnp.broadcast_to(jnp.sum(jnp.where(down == along, id_row, 0), axis=1, keepdims=True), (64, 64))
    same = id_row == id_col
    slot_row = jnp.sum(jnp.where(same & (down < along), 1, 0), axis=0, keepdims=True) * HOMES + ids
    slot_col = jnp.sum(jnp.where(same & (along < down), 1, 0), axis=1, keepdims=True) * HOMES + jnp.sum(
        jnp.where(down == along, id_row, 0), axis=1, keepdims=True
    )
    slot_col = jnp.broadcast_to(slot_col, (64, 64))
    slot_row = jnp.broadcast_to(slot_row, (64, 64))
    st[...] = jnp.concatenate([slot_row[0:8], jnp.full((8, 64), -1, jnp.int32)], axis=1)

    strain_cols = jnp.concatenate([strain_ref[...], jnp.zeros((122, 64), jnp.float32)], axis=0)
    for c in range(CHUNKS):
        pick = jnp.where(down + c * 64 == slot_row, 1.0, 0.0)
        for b in range(6):
            rows = jnp.dot(pick, state_ref[b], precision=HIGHEST, preferred_element_type=jnp.float32)
            for q in range(2):
                tx[c, pl.ds(b * 2 + q, HOMES, stride=MSG), :] = rows[q * 32 : (q + 1) * 32]
        rows = lax.dot_general(
            pick, strain_cols, (((1,), (1,)), ((), ())), precision=HIGHEST, preferred_element_type=jnp.float32
        )
        for q in range(2):
            tx[c, pl.ds(12 + q, HOMES, stride=MSG), :] = rows[q * 32 : (q + 1) * 32]
            tx[c, pl.ds(14 + q, HOMES, stride=MSG), :] = jnp.zeros((HOMES, 128), jnp.float32)
            ty[c, pl.ds(12 + q, HOMES, stride=MSG), :] = jnp.zeros((HOMES, 128), jnp.float32)
            ty[c, pl.ds(14 + q, HOMES, stride=MSG), :] = jnp.zeros((HOMES, 128), jnp.float32)
    pacc[...] = jnp.zeros((128, 128), jnp.float32)

    pl.semaphore_wait(barrier, 31 + 7)

    def exchange(src, dst, c, send_sem, recv_sem):
        def body(i, carry):
            to = far(i)
            pltpu.make_async_remote_copy(
                src_ref=src.at[c, pl.ds(pl.multiple_of(to * MSG, MSG), MSG), :],
                dst_ref=dst.at[c, pl.ds(pl.multiple_of(me * MSG, MSG), MSG), :],
                send_sem=send_sem.at[c],
                recv_sem=recv_sem.at[c],
                device_id=(micro, to),
                device_id_type=MESH,
            ).start()
            return carry

        lax.fori_loop(0, HOMES - 1, body, 0)
        own = pl.ds(pl.multiple_of(me * MSG, MSG), MSG)
        dst[c, own, :] = src[c, own, :]

    def drain(ref, sem):
        pltpu.make_async_copy(ref, ref, sem).wait()

    for c in range(CHUNKS):
        exchange(tx, rx, c, in_send, in_recv)
    for side in range(2):
        pltpu.make_async_remote_copy(
            src_ref=st,
            dst_ref=sn.at[1 - side],
            send_sem=s_send.at[side],
            recv_sem=s_recv.at[1 - side],
            device_id=(micro, lax.rem(me + HOMES - 1 + 2 * side, HOMES)),
            device_id_type=MESH,
        ).start()

    lam, mu, level = moduli_ref[0], moduli_ref[1], moduli_ref[2]
    hard = 4.0 * mu * mu / (level * level)
    flag = plastic_ref[...].astype(jnp.float32)
    fraction = fraction_ref[...]
    total = jnp.sum(fraction, axis=1, keepdims=True)

    def send(s, block, low, high, to, kind):
        pltpu.make_async_remote_copy(
            src_ref=g.at[s, block, low:high],
            dst_ref=g.at[s, block, low:high],
            send_sem=ag_send.at[s],
            recv_sem=ag_recv.at[s, kind],
            device_id=(to, me),
            device_id_type=MESH,
        ).start()

    def polarize(s, strain):
        stress, tr = law(strain, lam, mu, hard, flag)
        for a in range(6):
            tau = stress[a] - (tr + 2.0 * strain[a]) if a < 3 else stress[a] - 2.0 * strain[a]
            g[s, micro, a] = tau.astype(jnp.bfloat16)

    def share(d, carry):
        pltpu.make_async_remote_copy(
            src_ref=px.at[micro],
            dst_ref=px.at[micro],
            send_sem=p_send,
            recv_sem=p_recv,
            device_id=(lax.rem(micro + d, 8), me),
            device_id_type=MESH,
        ).start()
        return carry

    def period(p, carry):
        def partial(s, a, blocks):
            total_a = None
            for j in blocks:
                lanes = pl.ds(pl.multiple_of(j * 128, 128), 128)
                rows = jnp.concatenate([w[a, b, :, lanes] for b in range(6)], axis=1)
                columns = jnp.concatenate([g[s, j, b] for b in range(6)], axis=1)
                part = lax.dot_general(rows, columns, (((1,), (1,)), ((), ())), preferred_element_type=jnp.float32)
                total_a = part if total_a is None else total_a + part
            return total_a

        @pl.when(p < CHUNKS)
        def _():
            drain(rx.at[p, 0 : 31 * MSG], in_recv.at[p])
            strain = [
                jnp.concatenate([rx[p, pl.ds(b * 2 + q, HOMES, stride=MSG), :] for q in range(2)], axis=0)
                for b in range(6)
            ]
            tg[p] = jnp.concatenate([rx[p, pl.ds(12 + q, HOMES, stride=MSG), :] for q in range(2)], axis=0)
            polarize(p, strain)

        @pl.when(p >= 2)
        def _():
            s = p - 2
            drain(g.at[s, 0, 0:3], ag_recv.at[s, 3])
            drain(g.at[s, 0, 0:3], ag_recv.at[s, 4])

            @pl.when(s < STAGES - 1)
            def _():
                send(s, across_left, 0, 3, right, 5)
                send(s, across_right, 3, 6, left, 5)

        @pl.when(p < STAGES)
        def _():
            send(p, micro, 0, 6, right, 0)
            send(p, micro, 0, 6, left, 1)
            send(p, micro, 0, 6, across, 2)

        @pl.when(p >= 2)
        def _():
            s = p - 2

            @pl.when(p == 2)
            def _():
                load_w.wait()

            for a in range(6):
                acc[a] = partial(s, a, [micro, left, right, across])

        @pl.when((p >= 1) & (p < STAGES + 1))
        def _():
            s = p - 1
            drain(g.at[s, 0], ag_recv.at[s, 0])
            send(s, left, 0, 3, right, 5)
            send(s, left, 0, 3, across, 3)
            drain(g.at[s, 0], ag_recv.at[s, 1])
            send(s, right, 3, 6, left, 5)
            send(s, right, 3, 6, across, 4)
            drain(g.at[s, 0], ag_recv.at[s, 2])
            send(s, across, 0, 3, left, 5)
            send(s, across, 3, 6, right, 5)

            @pl.when(s == STAGES - 1)
            def _():
                send(s, across, 0, 6, xo * 2 + r, 5)


        @pl.when(p >= 2)
        def _():
            s = p - 2
            c = lax.rem(s, CHUNKS)
            drain(g.at[s, 0:3], ag_recv.at[s, 5])
            target = tg[c]
            for a in range(6):
                rest = partial(s, a, [xo * 2 + r, across_left, across_right, xo * 2 + (1 - r)])
                ebuf[a] = target[:, a : a + 1] - (acc[a] + rest).T
            strain = [ebuf[a] for a in range(6)]

            @pl.when(s < STAGES - CHUNKS)
            def _():
                polarize(s + CHUNKS, strain)

            @pl.when(s >= STAGES - CHUNKS)
            def _():
                stress, _ = law(strain, lam, mu, hard, flag)
                lane = lax.broadcasted_iota(jnp.int32, (ROWS, 128), 1)
                sums = pacc[0:ROWS]
                for a in range(6):
                    part = jnp.sum(stress[a] * fraction, axis=1, keepdims=True)
                    sums = jnp.where(lane == c * 8 + a, part, sums)
                pacc[0:ROWS] = sums

                @pl.when(s == STAGES - 1)
                def _():
                    rows = pacc[...].T[0 : 8 * CHUNKS]
                    row = lax.broadcasted_iota(jnp.int32, (8 * CHUNKS, 128), 0)
                    px[micro] = jnp.where(row == 6, total, rows)
                    lax.fori_loop(1, 8, share, 0)

                for b in range(6):
                    for q in range(2):
                        ty[c, pl.ds(b * 2 + q, HOMES, stride=MSG), :] = ebuf[b, q * 32 : (q + 1) * 32]
                exchange(ty, ry, c, out_send, out_recv)

        return carry

    lax.fori_loop(0, STAGES + 2, period, 0)

    drain(px.at[0:7], p_recv)
    sums = px[0]
    for i in range(1, 8):
        sums = sums + px[i]
    mean = sums / sums[6:7]
    mean = jnp.concatenate([mean, jnp.zeros((128 - 8 * CHUNKS, 128), jnp.float32)], axis=0).T
    for d in range(3):
        for q in range(2):
            part = mean[q * 32 : (q + 1) * 32]
            if d != 1:
                part = pltpu.roll(part, 1 if d == 0 else 31, 0)
            rt[pl.ds(d * 2 + q, HOMES, stride=8), :] = part
    for spare in (6, 7):
        rt[pl.ds(spare, HOMES, stride=8), :] = jnp.zeros((HOMES, 128), jnp.float32)

    def give(i, carry):
        to = far(i)
        pltpu.make_async_remote_copy(
            src_ref=rt.at[pl.ds(pl.multiple_of(to * 8, 8), 8), :],
            dst_ref=rr.at[pl.ds(pl.multiple_of(me * 8, 8), 8), :],
            send_sem=r_send,
            recv_sem=r_recv,
            device_id=(micro, to),
            device_id_type=MESH,
        ).start()
        return carry

    lax.fori_loop(0, HOMES - 1, give, 0)
    own = pl.ds(pl.multiple_of(me * 8, 8), 8)
    rr[own, :] = rt[own, :]

    for c in range(CHUNKS):
        drain(ry.at[c, 0 : 31 * MSG], out_recv.at[c])
        pick = jnp.where(along + c * 64 == slot_col, 1.0, 0.0)
        for b in range(6):
            rows = jnp.concatenate([ry[c, pl.ds(b * 2 + q, HOMES, stride=MSG), :] for q in range(2)], axis=0)
            part = jnp.dot(pick, rows, precision=HIGHEST, preferred_element_type=jnp.float32)
            home_ref[b] = part if c == 0 else home_ref[b] + part

    for side in range(2):
        drain(sn.at[side], s_recv.at[side])
    drain(rr.at[0 : 31 * 8], r_recv)
    slots = [sn[0][0:1], st[0:1], sn[1][0:1]]
    down2 = lax.broadcasted_iota(jnp.int32, (64, 128), 0)
    hom = []
    for d in range(3):
        rows = jnp.concatenate([rr[pl.ds(d * 2 + q, HOMES, stride=8), :] for q in range(2)], axis=0).T
        slab = jnp.zeros((8, 128), jnp.float32)
        for c in range(CHUNKS):
            pick = jnp.where(down2 + c * 64 == jnp.broadcast_to(slots[d], (64, 128)), 1.0, 0.0)
            slab = slab + jnp.dot(
                rows[c * 8 : (c + 1) * 8], pick, precision=HIGHEST, preferred_element_type=jnp.float32
            )
        hom.append(slab)
    here = hom[1]
    hom_ref[...] = here[0:6, 0:64]
    lane = lax.broadcasted_iota(jnp.int32, (8, 128), 1)
    along_x = 0.5 * (pltpu.roll(here, 120, 1) - pltpu.roll(here, 8, 1))
    above = jnp.where(lane % 8 == 7, 0.0, pltpu.roll(here, 127, 1))
    below = jnp.where(lane % 8 == 0, 0.0, pltpu.roll(here, 1, 1))
    along_y = 0.5 * (above - below)
    along_z = 0.5 * (jnp.where(me == HOMES - 1, 0.0, hom[2]) - jnp.where(me == 0, 0.0, hom[0]))
    res_x = along_x[0:1] + along_y[5:6] + along_z[4:5]
    res_y = along_x[5:6] + along_y[1:2] + along_z[3:4]
    res_z = along_x[4:5] + along_y[3:4] + along_z[2:3]
    res_ref[...] = jnp.concatenate([res_x, res_y, res_z], axis=0)[:, 0:64]

    for c in range(CHUNKS):
        drain(tx.at[c, 0 : 31 * MSG], in_send.at[c])
        drain(ty.at[c, 0 : 31 * MSG], out_send.at[c])
    for side in range(2):
        drain(st, s_send.at[side])

    def sent(s, carry):
        drain(g.at[s, 0:7], ag_send.at[s])
        return carry

    lax.fori_loop(0, STAGES, sent, 0)
    drain(px.at[0:7], p_send)
    drain(rt.at[0 : 31 * 8], r_send)


def local(interaction, cluster_moduli, cluster_fraction, plastic_flag, micro_id, macro_strain, cluster_state):
    vmem = pl.BlockSpec(memory_space=pltpu.VMEM)
    home, hom, res = pl.pallas_call(
        kernel,
        out_shape=(
            jax.ShapeDtypeStruct((6, 64, 128), jnp.float32),
            jax.ShapeDtypeStruct((6, 64), jnp.float32),
            jax.ShapeDtypeStruct((3, 64), jnp.float32),
        ),
        in_specs=[pl.BlockSpec(memory_space=pltpu.HBM)] * 7,
        out_specs=(vmem, vmem, vmem),
        scratch_shapes=[
            pltpu.VMEM((6, 6, 128, 1024), jnp.bfloat16),
            pltpu.VMEM((3, 1, 128), jnp.float32),
            pltpu.VMEM((1, 128), jnp.float32),
            pltpu.VMEM((1, 128), jnp.int32),
            pltpu.VMEM((1, 64), jnp.int32),
            pltpu.VMEM((6, 64), jnp.float32),
            pltpu.VMEM((6, 64, 128), jnp.float32),
            pltpu.VMEM((6, 128, ROWS), jnp.float32),
            pltpu.VMEM((STAGES, 8, 6, ROWS, 128), jnp.bfloat16),
            pltpu.VMEM((CHUNKS, HOMES * MSG, 128), jnp.float32),
            pltpu.VMEM((CHUNKS, HOMES * MSG, 128), jnp.float32),
            pltpu.VMEM((CHUNKS, HOMES * MSG, 128), jnp.float32),
            pltpu.VMEM((CHUNKS, HOMES * MSG, 128), jnp.float32),
            pltpu.VMEM((CHUNKS, ROWS, 128), jnp.float32),
            pltpu.VMEM((6, ROWS, 128), jnp.float32),
            pltpu.VMEM((128, 128), jnp.float32),
            pltpu.VMEM((8, 8 * CHUNKS, 128), jnp.float32),
            pltpu.VMEM((HOMES * 8, 128), jnp.float32),
            pltpu.VMEM((HOMES * 8, 128), jnp.float32),
            pltpu.VMEM((8, 128), jnp.int32),
            pltpu.VMEM((2, 8, 128), jnp.int32),
            pltpu.SemaphoreType.DMA,
            pltpu.SemaphoreType.DMA((6,)),
            pltpu.SemaphoreType.DMA((CHUNKS,)),
            pltpu.SemaphoreType.DMA((CHUNKS,)),
            pltpu.SemaphoreType.DMA((STAGES,)),
            pltpu.SemaphoreType.DMA((STAGES, 6)),
            pltpu.SemaphoreType.DMA((CHUNKS,)),
            pltpu.SemaphoreType.DMA((CHUNKS,)),
            pltpu.SemaphoreType.DMA,
            pltpu.SemaphoreType.DMA,
            pltpu.SemaphoreType.DMA,
            pltpu.SemaphoreType.DMA,
            pltpu.SemaphoreType.DMA((2,)),
            pltpu.SemaphoreType.DMA((2,)),
        ],
        compiler_params=pltpu.CompilerParams(
            collective_id=0, has_side_effects=True, vmem_limit_bytes=40 * 2**20
        ),
    )(
        jnp.transpose(interaction[0], (0, 2, 1, 3)),
        jnp.transpose(cluster_moduli, (1, 0, 2)),
        cluster_fraction,
        plastic_flag,
        micro_id.reshape(1, -1),
        macro_strain.T,
        jnp.transpose(cluster_state, (1, 0, 2)),
    )
    return jnp.transpose(home, (1, 0, 2)), hom, res


def solution(mesh):
    placed = (
        P("macro", None, "micro", None, None),
        P("macro", None, "micro"),
        P("macro", "micro"),
        P("macro", "micro"),
        P("macro", None),
        P("macro", None),
        P("macro", None, "micro"),
    )
    return jax.shard_map(
        local,
        mesh=mesh,
        in_specs=placed,
        out_specs=(P("macro", None, "micro"), P(None, "macro"), P(None, "macro")),
        check_vma=False,
    )
```

```python
import functools

import jax
import jax.numpy as jnp
from jax import lax
from jax.experimental import pallas as pl
from jax.experimental.pallas import tpu as pltpu
from jax.sharding import PartitionSpec as P

MESH = pl.DeviceIdType.MESH
HIGHEST = lax.Precision.HIGHEST
ITERS = 3
CHUNKS = 3
HOMES = 32
ROWS = 64
STAGES = ITERS * CHUNKS
MSG = 16


def law(strain, lam, mu, hard, flag):
    tr = strain[0] + strain[1] + strain[2]
    third = tr / 3.0
    dev = [strain[0] - third, strain[1] - third, strain[2] - third, strain[3], strain[4], strain[5]]
    square = (dev[0] * dev[0] + dev[1] * dev[1] + dev[2] * dev[2]) + 2.0 * (
        dev[3] * dev[3] + dev[4] * dev[4] + dev[5] * dev[5]
    )
    soft = lax.rsqrt(1.0 + hard * square)
    scale = 2.0 * (mu * (1.0 + flag * (soft - 1.0)))
    bulk = (lam + 2.0 * mu / 3.0) * tr
    return [scale * dev[a] + bulk if a < 3 else scale * dev[a] for a in range(6)], tr


def kernel(
    w_hbm, moduli_hbm, fraction_hbm, plastic_hbm, id_hbm, strain_hbm, state_hbm,
    home_ref, hom_ref, res_ref,
    w, moduli_ref, fraction_ref, plastic_ref, id_ref, strain_ref, state_ref, acc, g, tx, rx, ty, ry, tg, ebuf, pacc, px, rt, rr, st, sn,
    w_sem, i_sem, in_send, in_recv, ag_send, ag_recv, out_send, out_recv, p_send, p_recv, r_send, r_recv, s_send, s_recv,
):
    micro, me = lax.axis_index("micro"), lax.axis_index("macro")
    x, r = micro // 2, micro % 2
    xl, xr, xo = lax.rem(x + 3, 4), lax.rem(x + 1, 4), lax.rem(x + 2, 4)
    left, right, across = xl * 2 + r, xr * 2 + r, x * 2 + (1 - r)
    across_left, across_right = xl * 2 + (1 - r), xr * 2 + (1 - r)

    loads = [
        pltpu.make_async_copy(src, dst, i_sem.at[i])
        for i, (src, dst) in enumerate(
            [
                (id_hbm, id_ref), (state_hbm, state_ref), (strain_hbm, strain_ref),
                (moduli_hbm, moduli_ref), (fraction_hbm, fraction_ref), (plastic_hbm, plastic_ref),
            ]
        )
    ]
    for load in loads:
        load.start()
    load_w = pltpu.make_async_copy(w_hbm, w, w_sem)
    load_w.start()

    barrier = pltpu.get_barrier_semaphore()

    def far(i):
        half = (i + 1) // 2
        return lax.rem(me + HOMES + 16 + half * (1 - 2 * (i % 2)), HOMES)

    def greet_macro(i, carry):
        pl.semaphore_signal(barrier, inc=1, device_id=(micro, far(i)), device_id_type=MESH)
        return carry

    def greet_micro(d, carry):
        pl.semaphore_signal(barrier, inc=1, device_id=(lax.rem(micro + d, 8), me), device_id_type=MESH)
        return carry

    lax.fori_loop(0, HOMES - 1, greet_macro, 0)
    lax.fori_loop(1, 8, greet_micro, 0)

    for load in loads:
        load.wait()
    ids = id_ref[...]
    down = lax.broadcasted_iota(jnp.int32, (64, 64), 0)
    along = lax.broadcasted_iota(jnp.int32, (64, 64), 1)
    id_row = jnp.broadcast_to(ids, (64, 64))
    id_col = jnp.broadcast_to(jnp.sum(jnp.where(down == along, id_row, 0), axis=1, keepdims=True), (64, 64))
    same = id_row == id_col
    slot_row = jnp.sum(jnp.where(same & (down < along), 1, 0), axis=0, keepdims=True) * HOMES + ids
    slot_col = jnp.sum(jnp.where(same & (along < down), 1, 0), axis=1, keepdims=True) * HOMES + jnp.sum(
        jnp.where(down == along, id_row, 0), axis=1, keepdims=True
    )
    slot_col = jnp.broadcast_to(slot_col, (64, 64))
    slot_row = jnp.broadcast_to(slot_row, (64, 64))
    st[...] = jnp.concatenate([slot_row[0:8], jnp.full((8, 64), -1, jnp.int32)], axis=1)

    strain_cols = jnp.concatenate([strain_ref[...], jnp.zeros((122, 64), jnp.float32)], axis=0)
    for c in range(CHUNKS):
        pick = jnp.where(down + c * 64 == slot_row, 1.0, 0.0)
        for b in range(6):
            rows = jnp.dot(pick, state_ref[b], precision=HIGHEST, preferred_element_type=jnp.float32)
            for q in range(2):
                tx[c, pl.ds(b * 2 + q, HOMES, stride=MSG), :] = rows[q * 32 : (q + 1) * 32]
        rows = lax.dot_general(
            pick, strain_cols, (((1,), (1,)), ((), ())), precision=HIGHEST, preferred_element_type=jnp.float32
        )
        for q in range(2):
            tx[c, pl.ds(12 + q, HOMES, stride=MSG), :] = rows[q * 32 : (q + 1) * 32]
            tx[c, pl.ds(14 + q, HOMES, stride=MSG), :] = jnp.zeros((HOMES, 128), jnp.float32)
            ty[c, pl.ds(12 + q, HOMES, stride=MSG), :] = jnp.zeros((HOMES, 128), jnp.float32)
            ty[c, pl.ds(14 + q, HOMES, stride=MSG), :] = jnp.zeros((HOMES, 128), jnp.float32)
    pacc[...] = jnp.zeros((128, 128), jnp.float32)

    pl.semaphore_wait(barrier, 31 + 7)

    def exchange(src, dst, c, send_sem, recv_sem):
        def body(i, carry):
            to = far(i)
            pltpu.make_async_remote_copy(
                src_ref=src.at[c, pl.ds(pl.multiple_of(to * MSG, MSG), MSG), :],
                dst_ref=dst.at[c, pl.ds(pl.multiple_of(me * MSG, MSG), MSG), :],
                send_sem=send_sem.at[c],
                recv_sem=recv_sem.at[c],
                device_id=(micro, to),
                device_id_type=MESH,
            ).start()
            return carry

        lax.fori_loop(0, HOMES - 1, body, 0)
        own = pl.ds(pl.multiple_of(me * MSG, MSG), MSG)
        dst[c, own, :] = src[c, own, :]

    def drain(ref, sem):
        pltpu.make_async_copy(ref, ref, sem).wait()

    for c in range(CHUNKS):
        exchange(tx, rx, c, in_send, in_recv)
    for side in range(2):
        pltpu.make_async_remote_copy(
            src_ref=st,
            dst_ref=sn.at[1 - side],
            send_sem=s_send.at[side],
            recv_sem=s_recv.at[1 - side],
            device_id=(micro, lax.rem(me + HOMES - 1 + 2 * side, HOMES)),
            device_id_type=MESH,
        ).start()

    lam, mu, level = moduli_ref[0], moduli_ref[1], moduli_ref[2]
    hard = 4.0 * mu * mu / (level * level)
    flag = plastic_ref[...].astype(jnp.float32)
    fraction = fraction_ref[...]
    total = jnp.sum(fraction, axis=1, keepdims=True)

    def send(s, block, low, high, to, kind):
        pltpu.make_async_remote_copy(
            src_ref=g.at[s, block, low:high],
            dst_ref=g.at[s, block, low:high],
            send_sem=ag_send.at[s],
            recv_sem=ag_recv.at[s, kind],
            device_id=(to, me),
            device_id_type=MESH,
        ).start()

    def polarize(s, strain):
        stress, tr = law(strain, lam, mu, hard, flag)
        for a in range(6):
            tau = stress[a] - (tr + 2.0 * strain[a]) if a < 3 else stress[a] - 2.0 * strain[a]
            g[s, micro, a] = tau.astype(jnp.bfloat16)

    def share(d, carry):
        pltpu.make_async_remote_copy(
            src_ref=px.at[micro],
            dst_ref=px.at[micro],
            send_sem=p_send,
            recv_sem=p_recv,
            device_id=(lax.rem(micro + d, 8), me),
            device_id_type=MESH,
        ).start()
        return carry

    def period(p, carry):
        def partial(s, a, blocks):
            total_a = None
            for j in blocks:
                lanes = pl.ds(pl.multiple_of(j * 128, 128), 128)
                rows = jnp.concatenate([w[a, b, :, lanes] for b in range(6)], axis=1)
                columns = jnp.concatenate([g[s, j, b] for b in range(6)], axis=1)
                part = lax.dot_general(rows, columns, (((1,), (1,)), ((), ())), preferred_element_type=jnp.float32)
                total_a = part if total_a is None else total_a + part
            return total_a

        @pl.when(p < CHUNKS)
        def _():
            drain(rx.at[p, 0 : 31 * MSG], in_recv.at[p])
            strain = [
                jnp.concatenate([rx[p, pl.ds(b * 2 + q, HOMES, stride=MSG), :] for q in range(2)], axis=0)
                for b in range(6)
            ]
            tg[p] = jnp.concatenate([rx[p, pl.ds(12 + q, HOMES, stride=MSG), :] for q in range(2)], axis=0)
            polarize(p, strain)

        @pl.when(p >= 2)
        def _():
            s = p - 2
            drain(g.at[s, 0, 0:3], ag_recv.at[s, 3])
            drain(g.at[s, 0, 0:3], ag_recv.at[s, 4])

            @pl.when(s < STAGES - 1)
            def _():
                send(s, across_left, 0, 3, right, 5)
                send(s, across_right, 3, 6, left, 5)

        @pl.when(p < STAGES)
        def _():
            send(p, micro, 0, 6, right, 0)
            send(p, micro, 0, 6, left, 1)
            send(p, micro, 0, 6, across, 2)

        @pl.when(p >= 2)
        def _():
            s = p - 2

            @pl.when(p == 2)
            def _():
                load_w.wait()

            for a in range(6):
                acc[a] = partial(s, a, [micro, left, right, across])

        @pl.when((p >= 1) & (p < STAGES + 1))
        def _():
            s = p - 1
            drain(g.at[s, 0], ag_recv.at[s, 0])
            send(s, left, 0, 3, right, 5)
            send(s, left, 0, 3, across, 3)
            drain(g.at[s, 0], ag_recv.at[s, 1])
            send(s, right, 3, 6, left, 5)
            send(s, right, 3, 6, across, 4)
            drain(g.at[s, 0], ag_recv.at[s, 2])
            send(s, across, 0, 3, left, 5)
            send(s, across, 3, 6, right, 5)

            @pl.when(s == STAGES - 1)
            def _():
                send(s, across, 0, 6, xo * 2 + r, 5)


        @pl.when(p >= 2)
        def _():
            s = p - 2
            c = lax.rem(s, CHUNKS)
            drain(g.at[s, 0:3], ag_recv.at[s, 5])
            target = tg[c]
            for a in range(6):
                rest = partial(s, a, [xo * 2 + r, across_left, across_right, xo * 2 + (1 - r)])
                ebuf[a] = target[:, a : a + 1] - (acc[a] + rest).T
            strain = [ebuf[a] for a in range(6)]

            @pl.when(s < STAGES - CHUNKS)
            def _():
                polarize(s + CHUNKS, strain)

            @pl.when(s >= STAGES - CHUNKS)
            def _():
                stress, _ = law(strain, lam, mu, hard, flag)
                lane = lax.broadcasted_iota(jnp.int32, (ROWS, 128), 1)
                sums = pacc[0:ROWS]
                for a in range(6):
                    part = jnp.sum(stress[a] * fraction, axis=1, keepdims=True)
                    sums = jnp.where(lane == c * 8 + a, part, sums)
                pacc[0:ROWS] = sums

                @pl.when(s == STAGES - 1)
                def _():
                    rows = pacc[...].T[0 : 8 * CHUNKS]
                    row = lax.broadcasted_iota(jnp.int32, (8 * CHUNKS, 128), 0)
                    px[micro] = jnp.where(row == 6, total, rows)
                    lax.fori_loop(1, 8, share, 0)

                for b in range(6):
                    for q in range(2):
                        ty[c, pl.ds(b * 2 + q, HOMES, stride=MSG), :] = ebuf[b, q * 32 : (q + 1) * 32]
                exchange(ty, ry, c, out_send, out_recv)

        return carry

    lax.fori_loop(0, STAGES + 2, period, 0)

    drain(px.at[0:7], p_recv)
    sums = px[0]
    for i in range(1, 8):
        sums = sums + px[i]
    mean = sums / sums[6:7]
    mean = jnp.concatenate([mean, jnp.zeros((128 - 8 * CHUNKS, 128), jnp.float32)], axis=0).T
    for d in range(3):
        for q in range(2):
            part = mean[q * 32 : (q + 1) * 32]
            if d != 1:
                part = pltpu.roll(part, 1 if d == 0 else 31, 0)
            rt[pl.ds(d * 2 + q, HOMES, stride=8), :] = part
    for spare in (6, 7):
        rt[pl.ds(spare, HOMES, stride=8), :] = jnp.zeros((HOMES, 128), jnp.float32)

    def give(i, carry):
        to = far(i)
        pltpu.make_async_remote_copy(
            src_ref=rt.at[pl.ds(pl.multiple_of(to * 8, 8), 8), :],
            dst_ref=rr.at[pl.ds(pl.multiple_of(me * 8, 8), 8), :],
            send_sem=r_send,
            recv_sem=r_recv,
            device_id=(micro, to),
            device_id_type=MESH,
        ).start()
        return carry

    lax.fori_loop(0, HOMES - 1, give, 0)
    own = pl.ds(pl.multiple_of(me * 8, 8), 8)
    rr[own, :] = rt[own, :]

    for c in range(CHUNKS):
        drain(ry.at[c, 0 : 31 * MSG], out_recv.at[c])
        pick = jnp.where(along + c * 64 == slot_col, 1.0, 0.0)
        for b in range(6):
            rows = jnp.concatenate([ry[c, pl.ds(b * 2 + q, HOMES, stride=MSG), :] for q in range(2)], axis=0)
            part = jnp.dot(pick, rows, precision=HIGHEST, preferred_element_type=jnp.float32)
            home_ref[b] = part if c == 0 else home_ref[b] + part

    for side in range(2):
        drain(sn.at[side], s_recv.at[side])
    drain(rr.at[0 : 31 * 8], r_recv)
    slots = [sn[0][0:1], st[0:1], sn[1][0:1]]
    down2 = lax.broadcasted_iota(jnp.int32, (64, 128), 0)
    hom = []
    for d in range(3):
        rows = jnp.concatenate([rr[pl.ds(d * 2 + q, HOMES, stride=8), :] for q in range(2)], axis=0).T
        slab = jnp.zeros((8, 128), jnp.float32)
        for c in range(CHUNKS):
            pick = jnp.where(down2 + c * 64 == jnp.broadcast_to(slots[d], (64, 128)), 1.0, 0.0)
            slab = slab + jnp.dot(
                rows[c * 8 : (c + 1) * 8], pick, precision=HIGHEST, preferred_element_type=jnp.float32
            )
        hom.append(slab)
    here = hom[1]
    hom_ref[...] = here[0:6, 0:64]
    lane = lax.broadcasted_iota(jnp.int32, (8, 128), 1)
    along_x = 0.5 * (pltpu.roll(here, 120, 1) - pltpu.roll(here, 8, 1))
    above = jnp.where(lane % 8 == 7, 0.0, pltpu.roll(here, 127, 1))
    below = jnp.where(lane % 8 == 0, 0.0, pltpu.roll(here, 1, 1))
    along_y = 0.5 * (above - below)
    along_z = 0.5 * (jnp.where(me == HOMES - 1, 0.0, hom[2]) - jnp.where(me == 0, 0.0, hom[0]))
    res_x = along_x[0:1] + along_y[5:6] + along_z[4:5]
    res_y = along_x[5:6] + along_y[1:2] + along_z[3:4]
    res_z = along_x[4:5] + along_y[3:4] + along_z[2:3]
    res_ref[...] = jnp.concatenate([res_x, res_y, res_z], axis=0)[:, 0:64]

    for c in range(CHUNKS):
        drain(tx.at[c, 0 : 31 * MSG], in_send.at[c])
        drain(ty.at[c, 0 : 31 * MSG], out_send.at[c])
    for side in range(2):
        drain(st, s_send.at[side])

    def sent(s, carry):
        drain(g.at[s, 0:7], ag_send.at[s])
        return carry

    lax.fori_loop(0, STAGES, sent, 0)
    drain(px.at[0:7], p_send)
    drain(rt.at[0 : 31 * 8], r_send)


def local(interaction, cluster_moduli, cluster_fraction, plastic_flag, micro_id, macro_strain, cluster_state):
    vmem = pl.BlockSpec(memory_space=pltpu.VMEM)
    home, hom, res = pl.pallas_call(
        kernel,
        out_shape=(
            pltpu.VMEM((6, 64, 128), jnp.float32),
            pltpu.VMEM((6, 64), jnp.float32),
            pltpu.VMEM((3, 64), jnp.float32),
        ),
        in_specs=[pl.BlockSpec(memory_space=pl.ANY)] * 7,
        out_specs=(vmem, vmem, vmem),
        scratch_shapes=[
            pltpu.VMEM((6, 6, 128, 1024), jnp.bfloat16),
            pltpu.VMEM((3, 1, 128), jnp.float32),
            pltpu.VMEM((1, 128), jnp.float32),
            pltpu.VMEM((1, 128), jnp.int32),
            pltpu.VMEM((1, 64), jnp.int32),
            pltpu.VMEM((6, 64), jnp.float32),
            pltpu.VMEM((6, 64, 128), jnp.float32),
            pltpu.VMEM((6, 128, ROWS), jnp.float32),
            pltpu.VMEM((STAGES, 8, 6, ROWS, 128), jnp.bfloat16),
            pltpu.VMEM((CHUNKS, HOMES * MSG, 128), jnp.float32),
            pltpu.VMEM((CHUNKS, HOMES * MSG, 128), jnp.float32),
            pltpu.VMEM((CHUNKS, HOMES * MSG, 128), jnp.float32),
            pltpu.VMEM((CHUNKS, HOMES * MSG, 128), jnp.float32),
            pltpu.VMEM((CHUNKS, ROWS, 128), jnp.float32),
            pltpu.VMEM((6, ROWS, 128), jnp.float32),
            pltpu.VMEM((128, 128), jnp.float32),
            pltpu.VMEM((8, 8 * CHUNKS, 128), jnp.float32),
            pltpu.VMEM((HOMES * 8, 128), jnp.float32),
            pltpu.VMEM((HOMES * 8, 128), jnp.float32),
            pltpu.VMEM((8, 128), jnp.int32),
            pltpu.VMEM((2, 8, 128), jnp.int32),
            pltpu.SemaphoreType.DMA,
            pltpu.SemaphoreType.DMA((6,)),
            pltpu.SemaphoreType.DMA((CHUNKS,)),
            pltpu.SemaphoreType.DMA((CHUNKS,)),
            pltpu.SemaphoreType.DMA((STAGES,)),
            pltpu.SemaphoreType.DMA((STAGES, 6)),
            pltpu.SemaphoreType.DMA((CHUNKS,)),
            pltpu.SemaphoreType.DMA((CHUNKS,)),
            pltpu.SemaphoreType.DMA,
            pltpu.SemaphoreType.DMA,
            pltpu.SemaphoreType.DMA,
            pltpu.SemaphoreType.DMA,
            pltpu.SemaphoreType.DMA((2,)),
            pltpu.SemaphoreType.DMA((2,)),
        ],
        compiler_params=pltpu.CompilerParams(
            collective_id=0, has_side_effects=True, vmem_limit_bytes=56 * 2**20
        ),
    )(
        jnp.transpose(interaction[0], (0, 2, 1, 3)),
        jnp.transpose(cluster_moduli, (1, 0, 2)),
        cluster_fraction,
        plastic_flag,
        micro_id.reshape(1, -1),
        macro_strain.T,
        jnp.transpose(cluster_state, (1, 0, 2)),
    )
    return jnp.transpose(home, (1, 0, 2)), hom, res


def solution(mesh):
    placed = (
        P("macro", None, "micro", None, None),
        P("macro", None, "micro"),
        P("macro", "micro"),
        P("macro", "micro"),
        P("macro", None),
        P("macro", None),
        P("macro", None, "micro"),
    )
    return jax.shard_map(
        local,
        mesh=mesh,
        in_specs=placed,
        out_specs=(P("macro", None, "micro"), P(None, "macro"), P(None, "macro")),
        check_vma=False,
    )
```

```python
import functools

import jax
import jax.numpy as jnp
from jax import lax
from jax.experimental import pallas as pl
from jax.experimental.pallas import tpu as pltpu
from jax.sharding import PartitionSpec as P

MESH = pl.DeviceIdType.MESH
HIGHEST = lax.Precision.HIGHEST
ITERS = 3
LEVELS = 32767.0
STEPS = 32000.0
CHUNKS = 3
HOMES = 32
ROWS = 64
STAGES = ITERS * CHUNKS
MSG = 16


def law(strain, lam, mu, hard, flag):
    tr = strain[0] + strain[1] + strain[2]
    third = tr / 3.0
    dev = [strain[0] - third, strain[1] - third, strain[2] - third, strain[3], strain[4], strain[5]]
    square = (dev[0] * dev[0] + dev[1] * dev[1] + dev[2] * dev[2]) + 2.0 * (
        dev[3] * dev[3] + dev[4] * dev[4] + dev[5] * dev[5]
    )
    soft = lax.rsqrt(1.0 + hard * square)
    scale = 2.0 * (mu * (1.0 + flag * (soft - 1.0)))
    bulk = (lam + 2.0 * mu / 3.0) * tr
    return [scale * dev[a] + bulk if a < 3 else scale * dev[a] for a in range(6)], tr


def kernel(
    w_hbm, moduli_hbm, fraction_hbm, plastic_hbm, id_hbm, strain_hbm, state_hbm,
    home_ref, hom_ref, res_ref,
    w, moduli_ref, fraction_ref, plastic_ref, id_ref, strain_ref, state_ref, acc, g, tx, rx, ty, ry, ty16, ry16, tx16, rx16, tm, rm, tg, ebuf, pacc, px, rt, rr, st, sn,
    w_sem, i_sem, in_send, in_recv, ag_send, ag_recv, out_send, out_recv, p_send, p_recv, r_send, r_recv, m_send, m_recv, s_send, s_recv,
):
    micro, me = lax.axis_index("micro"), lax.axis_index("macro")
    x, r = micro // 2, micro % 2
    xl, xr, xo = lax.rem(x + 3, 4), lax.rem(x + 1, 4), lax.rem(x + 2, 4)
    left, right, across = xl * 2 + r, xr * 2 + r, x * 2 + (1 - r)
    across_left, across_right = xl * 2 + (1 - r), xr * 2 + (1 - r)

    loads = [
        pltpu.make_async_copy(src, dst, i_sem.at[i])
        for i, (src, dst) in enumerate(
            [
                (id_hbm, id_ref), (state_hbm, state_ref), (strain_hbm, strain_ref),
                (moduli_hbm, moduli_ref), (fraction_hbm, fraction_ref), (plastic_hbm, plastic_ref),
            ]
        )
    ]
    for load in loads:
        load.start()
    load_w = pltpu.make_async_copy(w_hbm, w, w_sem)
    load_w.start()

    barrier = pltpu.get_barrier_semaphore()

    def far(i):
        half = (i + 1) // 2
        return lax.rem(me + HOMES + 16 + half * (1 - 2 * (i % 2)), HOMES)

    def greet_macro(i, carry):
        pl.semaphore_signal(barrier, inc=1, device_id=(micro, far(i)), device_id_type=MESH)
        return carry

    def greet_micro(d, carry):
        pl.semaphore_signal(barrier, inc=1, device_id=(lax.rem(micro + d, 8), me), device_id_type=MESH)
        return carry

    lax.fori_loop(0, HOMES - 1, greet_macro, 0)
    lax.fori_loop(1, 8, greet_micro, 0)

    for load in loads:
        load.wait()
    ids = id_ref[...]
    down = lax.broadcasted_iota(jnp.int32, (64, 64), 0)
    along = lax.broadcasted_iota(jnp.int32, (64, 64), 1)
    id_row = jnp.broadcast_to(ids, (64, 64))
    id_col = jnp.broadcast_to(jnp.sum(jnp.where(down == along, id_row, 0), axis=1, keepdims=True), (64, 64))
    same = id_row == id_col
    slot_row = jnp.sum(jnp.where(same & (down < along), 1, 0), axis=0, keepdims=True) * HOMES + ids
    slot_col = jnp.sum(jnp.where(same & (along < down), 1, 0), axis=1, keepdims=True) * HOMES + jnp.sum(
        jnp.where(down == along, id_row, 0), axis=1, keepdims=True
    )
    slot_col = jnp.broadcast_to(slot_col, (64, 64))
    slot_row = jnp.broadcast_to(slot_row, (64, 64))
    st[...] = jnp.concatenate([slot_row[0:8], jnp.full((8, 64), -1, jnp.int32)], axis=1)

    strain_cols = jnp.concatenate([strain_ref[...], jnp.zeros((122, 64), jnp.float32)], axis=0)
    peak = jnp.abs(state_ref[0])
    for b in range(1, 6):
        peak = jnp.maximum(peak, jnp.abs(state_ref[b]))
    peak = jnp.maximum(jnp.max(peak, axis=1, keepdims=True), 1e-30)
    power = jnp.ceil(jnp.log2(peak))
    code = STEPS * jnp.exp2(-power)
    for b in range(6):
        state_ref[b] = jnp.round(state_ref[b] * code)
    power = jnp.broadcast_to(power, (64, 128))

    def fill(c):
        pick = jnp.where(down + c * 64 == slot_row, 1.0, 0.0)
        for b in range(7):
            rows = jnp.dot(
                pick, state_ref[b] if b < 6 else power, precision=HIGHEST, preferred_element_type=jnp.float32
            )
            for q in range(2):
                tx[c, pl.ds((b * 2 if b < 6 else 14) + q, HOMES, stride=MSG), :] = rows[q * 32 : (q + 1) * 32]
        rows = lax.dot_general(
            pick, strain_cols, (((1,), (1,)), ((), ())), precision=HIGHEST, preferred_element_type=jnp.float32
        )
        for q in range(2):
            tm[pl.ds(c * 2 + q, HOMES, stride=8), :] = rows[q * 32 : (q + 1) * 32]
            tx[c, pl.ds(12 + q, HOMES, stride=MSG), :] = jnp.zeros((HOMES, 128), jnp.float32)
            ty[c, pl.ds(12 + q, HOMES, stride=MSG), :] = jnp.zeros((HOMES, 128), jnp.float32)
            ty[c, pl.ds(14 + q, HOMES, stride=MSG), :] = jnp.zeros((HOMES, 128), jnp.float32)
        tx16[c] = tx[c].astype(jnp.int32).astype(jnp.int16)

    for c in range(CHUNKS):
        fill(c)
    for spare in (6, 7):
        tm[pl.ds(spare, HOMES, stride=8), :] = jnp.zeros((HOMES, 128), jnp.float32)
    pacc[...] = jnp.zeros((128, 128), jnp.float32)

    pl.semaphore_wait(barrier, 31 + 7)

    def exchange(src, dst, c, send_sem, recv_sem):
        def body(i, carry):
            to = far(i)
            pltpu.make_async_remote_copy(
                src_ref=src.at[c, pl.ds(pl.multiple_of(to * MSG, MSG), MSG), :],
                dst_ref=dst.at[c, pl.ds(pl.multiple_of(me * MSG, MSG), MSG), :],
                send_sem=send_sem.at[c],
                recv_sem=recv_sem.at[c],
                device_id=(micro, to),
                device_id_type=MESH,
            ).start()
            return carry

        lax.fori_loop(0, HOMES - 1, body, 0)
        own = pl.ds(pl.multiple_of(me * MSG, MSG), MSG)
        dst[c, own, :] = src[c, own, :]

    def drain(ref, sem):
        pltpu.make_async_copy(ref, ref, sem).wait()

    exchange(tx16, rx16, 0, in_send, in_recv)

    def aim(i, carry):
        to = far(i)
        pltpu.make_async_remote_copy(
            src_ref=tm.at[pl.ds(pl.multiple_of(to * 8, 8), 8), :],
            dst_ref=rm.at[pl.ds(pl.multiple_of(me * 8, 8), 8), :],
            send_sem=m_send,
            recv_sem=m_recv,
            device_id=(micro, to),
            device_id_type=MESH,
        ).start()
        return carry

    lax.fori_loop(0, HOMES - 1, aim, 0)
    own = pl.ds(pl.multiple_of(me * 8, 8), 8)
    rm[own, :] = tm[own, :]
    for c in range(1, CHUNKS):
        exchange(tx16, rx16, c, in_send, in_recv)
    for side in range(2):
        pltpu.make_async_remote_copy(
            src_ref=st,
            dst_ref=sn.at[1 - side],
            send_sem=s_send.at[side],
            recv_sem=s_recv.at[1 - side],
            device_id=(micro, lax.rem(me + HOMES - 1 + 2 * side, HOMES)),
            device_id_type=MESH,
        ).start()

    lam, mu, level = moduli_ref[0], moduli_ref[1], moduli_ref[2]
    hard = 4.0 * mu * mu / (level * level)
    flag = plastic_ref[...].astype(jnp.float32)
    fraction = fraction_ref[...]
    total = jnp.sum(fraction, axis=1, keepdims=True)

    def send(s, block, low, high, to, kind):
        pltpu.make_async_remote_copy(
            src_ref=g.at[s, block, low:high],
            dst_ref=g.at[s, block, low:high],
            send_sem=ag_send.at[s],
            recv_sem=ag_recv.at[s, kind],
            device_id=(to, me),
            device_id_type=MESH,
        ).start()

    def polarize(s, strain):
        stress, tr = law(strain, lam, mu, hard, flag)
        for a in range(6):
            tau = stress[a] - (tr + 2.0 * strain[a]) if a < 3 else stress[a] - 2.0 * strain[a]
            g[s, micro, a] = tau.astype(jnp.bfloat16)

    def share(d, carry):
        pltpu.make_async_remote_copy(
            src_ref=px.at[micro],
            dst_ref=px.at[micro],
            send_sem=p_send,
            recv_sem=p_recv,
            device_id=(lax.rem(micro + d, 8), me),
            device_id_type=MESH,
        ).start()
        return carry

    def period(p, carry):
        def partial(s, a, blocks):
            total_a = None
            for j in blocks:
                lanes = pl.ds(pl.multiple_of(j * 128, 128), 128)
                rows = jnp.concatenate([w[a, b, :, lanes] for b in range(6)], axis=1)
                columns = jnp.concatenate([g[s, j, b] for b in range(6)], axis=1)
                part = lax.dot_general(rows, columns, (((1,), (1,)), ((), ())), preferred_element_type=jnp.float32)
                total_a = part if total_a is None else total_a + part
            return total_a

        @pl.when(p < CHUNKS)
        def _():
            drain(rx16.at[p, 0 : 31 * MSG], in_recv.at[p])
            rx[p] = rx16[p].astype(jnp.int32).astype(jnp.float32)
            strain = [
                jnp.concatenate([rx[p, pl.ds(b * 2 + q, HOMES, stride=MSG), :] for q in range(2)], axis=0)
                for b in range(6)
            ]
            power = jnp.concatenate([rx[p, pl.ds(14 + q, HOMES, stride=MSG), :] for q in range(2)], axis=0)
            scale = jnp.exp2(power) * (1.0 / STEPS)
            polarize(p, [plane * scale for plane in strain])

        @pl.when(p >= 2)
        def _():
            s = p - 2
            drain(g.at[s, 0, 0:3], ag_recv.at[s, 3])
            drain(g.at[s, 0, 0:3], ag_recv.at[s, 4])

            @pl.when(s < STAGES - 1)
            def _():
                send(s, across_left, 0, 3, right, 5)
                send(s, across_right, 3, 6, left, 5)

        @pl.when(p < STAGES)
        def _():
            send(p, micro, 0, 6, right, 0)
            send(p, micro, 0, 6, left, 1)
            send(p, micro, 0, 6, across, 2)

        @pl.when(p >= 2)
        def _():
            s = p - 2

            @pl.when(p == 2)
            def _():
                load_w.wait()
                drain(rm.at[0 : 31 * 8], m_recv)
                for i in range(CHUNKS):
                    tg[i] = jnp.concatenate([rm[pl.ds(i * 2 + q, HOMES, stride=8), :] for q in range(2)], axis=0)

            for a in range(6):
                acc[a] = partial(s, a, [micro, left, right, across])

        @pl.when((p >= 1) & (p < STAGES + 1))
        def _():
            s = p - 1
            drain(g.at[s, 0], ag_recv.at[s, 0])
            send(s, left, 0, 3, right, 5)
            send(s, left, 0, 3, across, 3)
            drain(g.at[s, 0], ag_recv.at[s, 1])
            send(s, right, 3, 6, left, 5)
            send(s, right, 3, 6, across, 4)
            drain(g.at[s, 0], ag_recv.at[s, 2])
            send(s, across, 0, 3, left, 5)
            send(s, across, 3, 6, right, 5)

            @pl.when(s == STAGES - 1)
            def _():
                send(s, across, 0, 6, xo * 2 + r, 5)


        @pl.when(p >= 2)
        def _():
            s = p - 2
            c = lax.rem(s, CHUNKS)
            drain(g.at[s, 0:3], ag_recv.at[s, 5])
            target = tg[c]
            for a in range(6):
                rest = partial(s, a, [xo * 2 + r, across_left, across_right, xo * 2 + (1 - r)])
                ebuf[a] = target[:, a : a + 1] - (acc[a] + rest).T
            strain = [ebuf[a] for a in range(6)]

            @pl.when(s < STAGES - CHUNKS)
            def _():
                polarize(s + CHUNKS, strain)

            @pl.when(s >= STAGES - CHUNKS)
            def _():
                stress, _ = law(strain, lam, mu, hard, flag)
                lane = lax.broadcasted_iota(jnp.int32, (ROWS, 128), 1)
                sums = pacc[0:ROWS]
                for a in range(6):
                    part = jnp.sum(stress[a] * fraction, axis=1, keepdims=True)
                    sums = jnp.where(lane == c * 8 + a, part, sums)
                peak = jnp.abs(strain[0])
                for a in range(1, 6):
                    peak = jnp.maximum(peak, jnp.abs(strain[a]))
                peak = jnp.maximum(jnp.max(peak, axis=1, keepdims=True), 1e-30)
                pacc[0:ROWS] = jnp.where(lane == c * 8 + 7, peak, sums)
                code = LEVELS / peak

                @pl.when(s == STAGES - 1)
                def _():
                    rows = pacc[...].T[0 : 8 * CHUNKS]
                    row = lax.broadcasted_iota(jnp.int32, (8 * CHUNKS, 128), 0)
                    px[micro] = jnp.where(row == 6, total, rows)
                    lax.fori_loop(1, 8, share, 0)

                for b in range(6):
                    for q in range(2):
                        half = slice(q * 32, (q + 1) * 32)
                        ty[c, pl.ds(b * 2 + q, HOMES, stride=MSG), :] = strain[b][half] * code[half]
                ty16[c] = jnp.round(ty[c]).astype(jnp.int32).astype(jnp.int16)
                exchange(ty16, ry16, c, out_send, out_recv)

        return carry

    lax.fori_loop(0, STAGES + 2, period, 0)

    drain(px.at[0:7], p_recv)
    sums = px[0]
    for i in range(1, 8):
        sums = sums + px[i]
    row = lax.broadcasted_iota(jnp.int32, (8 * CHUNKS, 128), 0)
    mean = jnp.where(row % 8 == 7, px[micro], sums / sums[6:7])
    mean = jnp.concatenate([mean, jnp.zeros((128 - 8 * CHUNKS, 128), jnp.float32)], axis=0).T
    for d in range(3):
        for q in range(2):
            part = mean[q * 32 : (q + 1) * 32]
            if d != 1:
                part = pltpu.roll(part, 1 if d == 0 else 31, 0)
            rt[pl.ds(d * 2 + q, HOMES, stride=8), :] = part
    for spare in (6, 7):
        rt[pl.ds(spare, HOMES, stride=8), :] = jnp.zeros((HOMES, 128), jnp.float32)

    def give(i, carry):
        to = far(i)
        pltpu.make_async_remote_copy(
            src_ref=rt.at[pl.ds(pl.multiple_of(to * 8, 8), 8), :],
            dst_ref=rr.at[pl.ds(pl.multiple_of(me * 8, 8), 8), :],
            send_sem=r_send,
            recv_sem=r_recv,
            device_id=(micro, to),
            device_id_type=MESH,
        ).start()
        return carry

    lax.fori_loop(0, HOMES - 1, give, 0)
    own = pl.ds(pl.multiple_of(me * 8, 8), 8)
    rr[own, :] = rt[own, :]

    for c in range(CHUNKS):
        drain(ry16.at[c, 0 : 31 * MSG], out_recv.at[c])
        ry[c] = ry16[c].astype(jnp.int32).astype(jnp.float32)
        pick = jnp.where(along + c * 64 == slot_col, 1.0, 0.0)
        for b in range(6):
            rows = jnp.concatenate([ry[c, pl.ds(b * 2 + q, HOMES, stride=MSG), :] for q in range(2)], axis=0)
            part = jnp.dot(pick, rows, precision=HIGHEST, preferred_element_type=jnp.float32)
            home_ref[b] = part if c == 0 else home_ref[b] + part

    for side in range(2):
        drain(sn.at[side], s_recv.at[side])
    drain(rr.at[0 : 31 * 8], r_recv)
    peaks = jnp.concatenate([rr[pl.ds(2 + q, HOMES, stride=8), :] for q in range(2)], axis=0)
    scale = jnp.zeros((64, 1), jnp.float32)
    for c in range(CHUNKS):
        pick = jnp.where(along + c * 64 == slot_col, 1.0, 0.0)
        found = jnp.dot(pick, peaks, precision=HIGHEST, preferred_element_type=jnp.float32)
        scale = scale + found[:, c * 8 + 7 : c * 8 + 8]
    scale = scale * (1.0 / LEVELS)
    for b in range(6):
        home_ref[b] = home_ref[b] * scale
    slots = [sn[0][0:1], st[0:1], sn[1][0:1]]
    down2 = lax.broadcasted_iota(jnp.int32, (64, 128), 0)
    hom = []
    for d in range(3):
        rows = jnp.concatenate([rr[pl.ds(d * 2 + q, HOMES, stride=8), :] for q in range(2)], axis=0).T
        slab = jnp.zeros((8, 128), jnp.float32)
        for c in range(CHUNKS):
            pick = jnp.where(down2 + c * 64 == jnp.broadcast_to(slots[d], (64, 128)), 1.0, 0.0)
            slab = slab + jnp.dot(
                rows[c * 8 : (c + 1) * 8], pick, precision=HIGHEST, preferred_element_type=jnp.float32
            )
        hom.append(slab)
    here = hom[1]
    hom_ref[...] = here[0:6, 0:64]
    lane = lax.broadcasted_iota(jnp.int32, (8, 128), 1)
    along_x = 0.5 * (pltpu.roll(here, 120, 1) - pltpu.roll(here, 8, 1))
    above = jnp.where(lane % 8 == 7, 0.0, pltpu.roll(here, 127, 1))
    below = jnp.where(lane % 8 == 0, 0.0, pltpu.roll(here, 1, 1))
    along_y = 0.5 * (above - below)
    along_z = 0.5 * (jnp.where(me == HOMES - 1, 0.0, hom[2]) - jnp.where(me == 0, 0.0, hom[0]))
    res_x = along_x[0:1] + along_y[5:6] + along_z[4:5]
    res_y = along_x[5:6] + along_y[1:2] + along_z[3:4]
    res_z = along_x[4:5] + along_y[3:4] + along_z[2:3]
    res_ref[...] = jnp.concatenate([res_x, res_y, res_z], axis=0)[:, 0:64]

    for c in range(CHUNKS):
        drain(tx16.at[c, 0 : 31 * MSG], in_send.at[c])
        drain(ty16.at[c, 0 : 31 * MSG], out_send.at[c])
    for side in range(2):
        drain(st, s_send.at[side])

    def sent(s, carry):
        drain(g.at[s, 0:7], ag_send.at[s])
        return carry

    lax.fori_loop(0, STAGES, sent, 0)
    drain(px.at[0:7], p_send)
    drain(tm.at[0 : 31 * 8], m_send)
    drain(rt.at[0 : 31 * 8], r_send)


def local(interaction, cluster_moduli, cluster_fraction, plastic_flag, micro_id, macro_strain, cluster_state):
    vmem = pl.BlockSpec(memory_space=pltpu.VMEM)
    home, hom, res = pl.pallas_call(
        kernel,
        out_shape=(
            pltpu.VMEM((6, 64, 128), jnp.float32),
            pltpu.VMEM((6, 64), jnp.float32),
            pltpu.VMEM((3, 64), jnp.float32),
        ),
        in_specs=[pl.BlockSpec(memory_space=pl.ANY)] * 7,
        out_specs=(vmem, vmem, vmem),
        scratch_shapes=[
            pltpu.VMEM((6, 6, 128, 1024), jnp.bfloat16),
            pltpu.VMEM((3, 1, 128), jnp.float32),
            pltpu.VMEM((1, 128), jnp.float32),
            pltpu.VMEM((1, 128), jnp.int32),
            pltpu.VMEM((1, 64), jnp.int32),
            pltpu.VMEM((6, 64), jnp.float32),
            pltpu.VMEM((6, 64, 128), jnp.float32),
            pltpu.VMEM((6, 128, ROWS), jnp.float32),
            pltpu.VMEM((STAGES, 8, 6, ROWS, 128), jnp.bfloat16),
            pltpu.VMEM((CHUNKS, HOMES * MSG, 128), jnp.float32),
            pltpu.VMEM((CHUNKS, HOMES * MSG, 128), jnp.float32),
            pltpu.VMEM((CHUNKS, HOMES * MSG, 128), jnp.float32),
            pltpu.VMEM((CHUNKS, HOMES * MSG, 128), jnp.float32),
            pltpu.VMEM((CHUNKS, HOMES * MSG, 128), jnp.int16),
            pltpu.VMEM((CHUNKS, HOMES * MSG, 128), jnp.int16),
            pltpu.VMEM((CHUNKS, HOMES * MSG, 128), jnp.int16),
            pltpu.VMEM((CHUNKS, HOMES * MSG, 128), jnp.int16),
            pltpu.VMEM((HOMES * 8, 128), jnp.float32),
            pltpu.VMEM((HOMES * 8, 128), jnp.float32),
            pltpu.VMEM((CHUNKS, ROWS, 128), jnp.float32),
            pltpu.VMEM((6, ROWS, 128), jnp.float32),
            pltpu.VMEM((128, 128), jnp.float32),
            pltpu.VMEM((8, 8 * CHUNKS, 128), jnp.float32),
            pltpu.VMEM((HOMES * 8, 128), jnp.float32),
            pltpu.VMEM((HOMES * 8, 128), jnp.float32),
            pltpu.VMEM((8, 128), jnp.int32),
            pltpu.VMEM((2, 8, 128), jnp.int32),
            pltpu.SemaphoreType.DMA,
            pltpu.SemaphoreType.DMA((6,)),
            pltpu.SemaphoreType.DMA((CHUNKS,)),
            pltpu.SemaphoreType.DMA((CHUNKS,)),
            pltpu.SemaphoreType.DMA((STAGES,)),
            pltpu.SemaphoreType.DMA((STAGES, 6)),
            pltpu.SemaphoreType.DMA((CHUNKS,)),
            pltpu.SemaphoreType.DMA((CHUNKS,)),
            pltpu.SemaphoreType.DMA,
            pltpu.SemaphoreType.DMA,
            pltpu.SemaphoreType.DMA,
            pltpu.SemaphoreType.DMA,
            pltpu.SemaphoreType.DMA,
            pltpu.SemaphoreType.DMA,
            pltpu.SemaphoreType.DMA((2,)),
            pltpu.SemaphoreType.DMA((2,)),
        ],
        compiler_params=pltpu.CompilerParams(
            collective_id=0, has_side_effects=True, vmem_limit_bytes=56 * 2**20
        ),
    )(
        jnp.transpose(interaction[0], (0, 2, 1, 3)),
        jnp.transpose(cluster_moduli, (1, 0, 2)),
        cluster_fraction,
        plastic_flag,
        micro_id.reshape(1, -1),
        macro_strain.T,
        jnp.transpose(cluster_state, (1, 0, 2)),
    )
    return jnp.transpose(home, (1, 0, 2)), hom, res


def solution(mesh):
    placed = (
        P("macro", None, "micro", None, None),
        P("macro", None, "micro"),
        P("macro", "micro"),
        P("macro", "micro"),
        P("macro", None),
        P("macro", None),
        P("macro", None, "micro"),
    )
    return jax.shard_map(
        local,
        mesh=mesh,
        in_specs=placed,
        out_specs=(P("macro", None, "micro"), P(None, "macro"), P(None, "macro")),
        check_vma=False,
    )
```

```python
import functools

import jax
import jax.numpy as jnp
from jax import lax
from jax.experimental import pallas as pl
from jax.experimental.pallas import tpu as pltpu
from jax.sharding import PartitionSpec as P

MESH = pl.DeviceIdType.MESH
HIGHEST = lax.Precision.HIGHEST
ITERS = 3
LEVELS = 32767.0
CHUNKS = 3
HOMES = 32
ROWS = 64
STAGES = ITERS * CHUNKS
MSG = 16


def law(strain, lam, mu, hard, flag):
    tr = strain[0] + strain[1] + strain[2]
    third = tr / 3.0
    dev = [strain[0] - third, strain[1] - third, strain[2] - third, strain[3], strain[4], strain[5]]
    square = (dev[0] * dev[0] + dev[1] * dev[1] + dev[2] * dev[2]) + 2.0 * (
        dev[3] * dev[3] + dev[4] * dev[4] + dev[5] * dev[5]
    )
    soft = lax.rsqrt(1.0 + hard * square)
    scale = 2.0 * (mu * (1.0 + flag * (soft - 1.0)))
    bulk = (lam + 2.0 * mu / 3.0) * tr
    return [scale * dev[a] + bulk if a < 3 else scale * dev[a] for a in range(6)], tr


def kernel(
    w_hbm, moduli_hbm, fraction_hbm, plastic_hbm, id_hbm, strain_hbm, state_hbm,
    home_ref, hom_ref, res_ref,
    w, moduli_ref, fraction_ref, plastic_ref, id_ref, strain_ref, state_ref, acc, g, tx, rx, ty, ry, ty16, ry16, tg, ebuf, pacc, px, rt, rr, st, sn,
    w_sem, i_sem, in_send, in_recv, ag_send, ag_recv, out_send, out_recv, p_send, p_recv, r_send, r_recv, s_send, s_recv,
):
    micro, me = lax.axis_index("micro"), lax.axis_index("macro")
    x, r = micro // 2, micro % 2
    xl, xr, xo = lax.rem(x + 3, 4), lax.rem(x + 1, 4), lax.rem(x + 2, 4)
    left, right, across = xl * 2 + r, xr * 2 + r, x * 2 + (1 - r)
    across_left, across_right = xl * 2 + (1 - r), xr * 2 + (1 - r)

    loads = [
        pltpu.make_async_copy(src, dst, i_sem.at[i])
        for i, (src, dst) in enumerate(
            [
                (id_hbm, id_ref), (state_hbm, state_ref), (strain_hbm, strain_ref),
                (moduli_hbm, moduli_ref), (fraction_hbm, fraction_ref), (plastic_hbm, plastic_ref),
            ]
        )
    ]
    for load in loads:
        load.start()
    load_w = pltpu.make_async_copy(w_hbm, w, w_sem)
    load_w.start()

    barrier = pltpu.get_barrier_semaphore()

    def far(i):
        half = (i + 1) // 2
        return lax.rem(me + HOMES + 16 + half * (1 - 2 * (i % 2)), HOMES)

    def greet_macro(i, carry):
        pl.semaphore_signal(barrier, inc=1, device_id=(micro, far(i)), device_id_type=MESH)
        return carry

    def greet_micro(d, carry):
        pl.semaphore_signal(barrier, inc=1, device_id=(lax.rem(micro + d, 8), me), device_id_type=MESH)
        return carry

    lax.fori_loop(0, HOMES - 1, greet_macro, 0)
    lax.fori_loop(1, 8, greet_micro, 0)

    for load in loads:
        load.wait()
    ids = id_ref[...]
    down = lax.broadcasted_iota(jnp.int32, (64, 64), 0)
    along = lax.broadcasted_iota(jnp.int32, (64, 64), 1)
    id_row = jnp.broadcast_to(ids, (64, 64))
    id_col = jnp.broadcast_to(jnp.sum(jnp.where(down == along, id_row, 0), axis=1, keepdims=True), (64, 64))
    same = id_row == id_col
    slot_row = jnp.sum(jnp.where(same & (down < along), 1, 0), axis=0, keepdims=True) * HOMES + ids
    slot_col = jnp.sum(jnp.where(same & (along < down), 1, 0), axis=1, keepdims=True) * HOMES + jnp.sum(
        jnp.where(down == along, id_row, 0), axis=1, keepdims=True
    )
    slot_col = jnp.broadcast_to(slot_col, (64, 64))
    slot_row = jnp.broadcast_to(slot_row, (64, 64))
    st[...] = jnp.concatenate([slot_row[0:8], jnp.full((8, 64), -1, jnp.int32)], axis=1)

    strain_cols = jnp.concatenate([strain_ref[...], jnp.zeros((122, 64), jnp.float32)], axis=0)
    def fill(c):
        pick = jnp.where(down + c * 64 == slot_row, 1.0, 0.0)
        for b in range(6):
            rows = jnp.dot(pick, state_ref[b], precision=HIGHEST, preferred_element_type=jnp.float32)
            for q in range(2):
                tx[c, pl.ds(b * 2 + q, HOMES, stride=MSG), :] = rows[q * 32 : (q + 1) * 32]
        rows = lax.dot_general(
            pick, strain_cols, (((1,), (1,)), ((), ())), precision=HIGHEST, preferred_element_type=jnp.float32
        )
        for q in range(2):
            tx[c, pl.ds(12 + q, HOMES, stride=MSG), :] = rows[q * 32 : (q + 1) * 32]
            tx[c, pl.ds(14 + q, HOMES, stride=MSG), :] = jnp.zeros((HOMES, 128), jnp.float32)
            ty[c, pl.ds(12 + q, HOMES, stride=MSG), :] = jnp.zeros((HOMES, 128), jnp.float32)
            ty[c, pl.ds(14 + q, HOMES, stride=MSG), :] = jnp.zeros((HOMES, 128), jnp.float32)

    fill(0)
    pacc[...] = jnp.zeros((128, 128), jnp.float32)

    pl.semaphore_wait(barrier, 31 + 7)

    def exchange(src, dst, c, send_sem, recv_sem):
        def body(i, carry):
            to = far(i)
            pltpu.make_async_remote_copy(
                src_ref=src.at[c, pl.ds(pl.multiple_of(to * MSG, MSG), MSG), :],
                dst_ref=dst.at[c, pl.ds(pl.multiple_of(me * MSG, MSG), MSG), :],
                send_sem=send_sem.at[c],
                recv_sem=recv_sem.at[c],
                device_id=(micro, to),
                device_id_type=MESH,
            ).start()
            return carry

        lax.fori_loop(0, HOMES - 1, body, 0)
        own = pl.ds(pl.multiple_of(me * MSG, MSG), MSG)
        dst[c, own, :] = src[c, own, :]

    def drain(ref, sem):
        pltpu.make_async_copy(ref, ref, sem).wait()

    exchange(tx, rx, 0, in_send, in_recv)
    for c in range(1, CHUNKS):
        fill(c)
        exchange(tx, rx, c, in_send, in_recv)
    for side in range(2):
        pltpu.make_async_remote_copy(
            src_ref=st,
            dst_ref=sn.at[1 - side],
            send_sem=s_send.at[side],
            recv_sem=s_recv.at[1 - side],
            device_id=(micro, lax.rem(me + HOMES - 1 + 2 * side, HOMES)),
            device_id_type=MESH,
        ).start()

    lam, mu, level = moduli_ref[0], moduli_ref[1], moduli_ref[2]
    hard = 4.0 * mu * mu / (level * level)
    flag = plastic_ref[...].astype(jnp.float32)
    fraction = fraction_ref[...]
    total = jnp.sum(fraction, axis=1, keepdims=True)

    def send(s, block, low, high, to, kind):
        pltpu.make_async_remote_copy(
            src_ref=g.at[s, block, low:high],
            dst_ref=g.at[s, block, low:high],
            send_sem=ag_send.at[s],
            recv_sem=ag_recv.at[s, kind],
            device_id=(to, me),
            device_id_type=MESH,
        ).start()

    def polarize(s, strain):
        stress, tr = law(strain, lam, mu, hard, flag)
        for a in range(6):
            tau = stress[a] - (tr + 2.0 * strain[a]) if a < 3 else stress[a] - 2.0 * strain[a]
            g[s, micro, a] = tau.astype(jnp.bfloat16)

    def share(d, carry):
        pltpu.make_async_remote_copy(
            src_ref=px.at[micro],
            dst_ref=px.at[micro],
            send_sem=p_send,
            recv_sem=p_recv,
            device_id=(lax.rem(micro + d, 8), me),
            device_id_type=MESH,
        ).start()
        return carry

    def period(p, carry):
        def partial(s, a, blocks):
            total_a = None
            for j in blocks:
                lanes = pl.ds(pl.multiple_of(j * 128, 128), 128)
                rows = jnp.concatenate([w[a, b, :, lanes] for b in range(6)], axis=1)
                columns = jnp.concatenate([g[s, j, b] for b in range(6)], axis=1)
                part = lax.dot_general(rows, columns, (((1,), (1,)), ((), ())), preferred_element_type=jnp.float32)
                total_a = part if total_a is None else total_a + part
            return total_a

        @pl.when(p < CHUNKS)
        def _():
            drain(rx.at[p, 0 : 31 * MSG], in_recv.at[p])
            strain = [
                jnp.concatenate([rx[p, pl.ds(b * 2 + q, HOMES, stride=MSG), :] for q in range(2)], axis=0)
                for b in range(6)
            ]
            tg[p] = jnp.concatenate([rx[p, pl.ds(12 + q, HOMES, stride=MSG), :] for q in range(2)], axis=0)
            polarize(p, strain)

        @pl.when(p >= 2)
        def _():
            s = p - 2
            drain(g.at[s, 0, 0:3], ag_recv.at[s, 3])
            drain(g.at[s, 0, 0:3], ag_recv.at[s, 4])

            @pl.when(s < STAGES - 1)
            def _():
                send(s, across_left, 0, 3, right, 5)
                send(s, across_right, 3, 6, left, 5)

        @pl.when(p < STAGES)
        def _():
            send(p, micro, 0, 6, right, 0)
            send(p, micro, 0, 6, left, 1)
            send(p, micro, 0, 6, across, 2)

        @pl.when(p >= 2)
        def _():
            s = p - 2

            @pl.when(p == 2)
            def _():
                load_w.wait()

            for a in range(6):
                acc[a] = partial(s, a, [micro, left, right, across])

        @pl.when((p >= 1) & (p < STAGES + 1))
        def _():
            s = p - 1
            drain(g.at[s, 0], ag_recv.at[s, 0])
            send(s, left, 0, 3, right, 5)
            send(s, left, 0, 3, across, 3)
            drain(g.at[s, 0], ag_recv.at[s, 1])
            send(s, right, 3, 6, left, 5)
            send(s, right, 3, 6, across, 4)
            drain(g.at[s, 0], ag_recv.at[s, 2])
            send(s, across, 0, 3, left, 5)
            send(s, across, 3, 6, right, 5)

            @pl.when(s == STAGES - 1)
            def _():
                send(s, across, 0, 6, xo * 2 + r, 5)


        @pl.when(p >= 2)
        def _():
            s = p - 2
            c = lax.rem(s, CHUNKS)
            drain(g.at[s, 0:3], ag_recv.at[s, 5])
            target = tg[c]
            for a in range(6):
                rest = partial(s, a, [xo * 2 + r, across_left, across_right, xo * 2 + (1 - r)])
                ebuf[a] = target[:, a : a + 1] - (acc[a] + rest).T
            strain = [ebuf[a] for a in range(6)]

            @pl.when(s < STAGES - CHUNKS)
            def _():
                polarize(s + CHUNKS, strain)

            @pl.when(s >= STAGES - CHUNKS)
            def _():
                stress, _ = law(strain, lam, mu, hard, flag)
                lane = lax.broadcasted_iota(jnp.int32, (ROWS, 128), 1)
                sums = pacc[0:ROWS]
                for a in range(6):
                    part = jnp.sum(stress[a] * fraction, axis=1, keepdims=True)
                    sums = jnp.where(lane == c * 8 + a, part, sums)
                peak = jnp.abs(strain[0])
                for a in range(1, 6):
                    peak = jnp.maximum(peak, jnp.abs(strain[a]))
                peak = jnp.maximum(jnp.max(peak, axis=1, keepdims=True), 1e-30)
                pacc[0:ROWS] = jnp.where(lane == c * 8 + 7, peak, sums)
                code = LEVELS / peak

                @pl.when(s == STAGES - 1)
                def _():
                    rows = pacc[...].T[0 : 8 * CHUNKS]
                    row = lax.broadcasted_iota(jnp.int32, (8 * CHUNKS, 128), 0)
                    px[micro] = jnp.where(row == 6, total, rows)
                    lax.fori_loop(1, 8, share, 0)

                for b in range(6):
                    for q in range(2):
                        half = slice(q * 32, (q + 1) * 32)
                        ty[c, pl.ds(b * 2 + q, HOMES, stride=MSG), :] = strain[b][half] * code[half]
                ty16[c] = jnp.round(ty[c]).astype(jnp.int32).astype(jnp.int16)
                exchange(ty16, ry16, c, out_send, out_recv)

        return carry

    lax.fori_loop(0, STAGES + 2, period, 0)

    drain(px.at[0:7], p_recv)
    sums = px[0]
    for i in range(1, 8):
        sums = sums + px[i]
    row = lax.broadcasted_iota(jnp.int32, (8 * CHUNKS, 128), 0)
    mean = jnp.where(row % 8 == 7, px[micro], sums / sums[6:7])
    mean = jnp.concatenate([mean, jnp.zeros((128 - 8 * CHUNKS, 128), jnp.float32)], axis=0).T
    for d in range(3):
        for q in range(2):
            part = mean[q * 32 : (q + 1) * 32]
            if d != 1:
                part = pltpu.roll(part, 1 if d == 0 else 31, 0)
            rt[pl.ds(d * 2 + q, HOMES, stride=8), :] = part
    for spare in (6, 7):
        rt[pl.ds(spare, HOMES, stride=8), :] = jnp.zeros((HOMES, 128), jnp.float32)

    def give(i, carry):
        to = far(i)
        pltpu.make_async_remote_copy(
            src_ref=rt.at[pl.ds(pl.multiple_of(to * 8, 8), 8), :],
            dst_ref=rr.at[pl.ds(pl.multiple_of(me * 8, 8), 8), :],
            send_sem=r_send,
            recv_sem=r_recv,
            device_id=(micro, to),
            device_id_type=MESH,
        ).start()
        return carry

    lax.fori_loop(0, HOMES - 1, give, 0)
    own = pl.ds(pl.multiple_of(me * 8, 8), 8)
    rr[own, :] = rt[own, :]

    for c in range(CHUNKS):
        drain(ry16.at[c, 0 : 31 * MSG], out_recv.at[c])
        ry[c] = ry16[c].astype(jnp.int32).astype(jnp.float32)
        pick = jnp.where(along + c * 64 == slot_col, 1.0, 0.0)
        for b in range(6):
            rows = jnp.concatenate([ry[c, pl.ds(b * 2 + q, HOMES, stride=MSG), :] for q in range(2)], axis=0)
            part = jnp.dot(pick, rows, precision=HIGHEST, preferred_element_type=jnp.float32)
            home_ref[b] = part if c == 0 else home_ref[b] + part

    for side in range(2):
        drain(sn.at[side], s_recv.at[side])
    drain(rr.at[0 : 31 * 8], r_recv)
    peaks = jnp.concatenate([rr[pl.ds(2 + q, HOMES, stride=8), :] for q in range(2)], axis=0)
    scale = jnp.zeros((64, 1), jnp.float32)
    for c in range(CHUNKS):
        pick = jnp.where(along + c * 64 == slot_col, 1.0, 0.0)
        found = jnp.dot(pick, peaks, precision=HIGHEST, preferred_element_type=jnp.float32)
        scale = scale + found[:, c * 8 + 7 : c * 8 + 8]
    scale = scale * (1.0 / LEVELS)
    for b in range(6):
        home_ref[b] = home_ref[b] * scale
    slots = [sn[0][0:1], st[0:1], sn[1][0:1]]
    down2 = lax.broadcasted_iota(jnp.int32, (64, 128), 0)
    hom = []
    for d in range(3):
        rows = jnp.concatenate([rr[pl.ds(d * 2 + q, HOMES, stride=8), :] for q in range(2)], axis=0).T
        slab = jnp.zeros((8, 128), jnp.float32)
        for c in range(CHUNKS):
            pick = jnp.where(down2 + c * 64 == jnp.broadcast_to(slots[d], (64, 128)), 1.0, 0.0)
            slab = slab + jnp.dot(
                rows[c * 8 : (c + 1) * 8], pick, precision=HIGHEST, preferred_element_type=jnp.float32
            )
        hom.append(slab)
    here = hom[1]
    hom_ref[...] = here[0:6, 0:64]
    lane = lax.broadcasted_iota(jnp.int32, (8, 128), 1)
    along_x = 0.5 * (pltpu.roll(here, 120, 1) - pltpu.roll(here, 8, 1))
    above = jnp.where(lane % 8 == 7, 0.0, pltpu.roll(here, 127, 1))
    below = jnp.where(lane % 8 == 0, 0.0, pltpu.roll(here, 1, 1))
    along_y = 0.5 * (above - below)
    along_z = 0.5 * (jnp.where(me == HOMES - 1, 0.0, hom[2]) - jnp.where(me == 0, 0.0, hom[0]))
    res_x = along_x[0:1] + along_y[5:6] + along_z[4:5]
    res_y = along_x[5:6] + along_y[1:2] + along_z[3:4]
    res_z = along_x[4:5] + along_y[3:4] + along_z[2:3]
    res_ref[...] = jnp.concatenate([res_x, res_y, res_z], axis=0)[:, 0:64]

    for c in range(CHUNKS):
        drain(tx.at[c, 0 : 31 * MSG], in_send.at[c])
        drain(ty16.at[c, 0 : 31 * MSG], out_send.at[c])
    for side in range(2):
        drain(st, s_send.at[side])

    def sent(s, carry):
        drain(g.at[s, 0:7], ag_send.at[s])
        return carry

    lax.fori_loop(0, STAGES, sent, 0)
    drain(px.at[0:7], p_send)
    drain(rt.at[0 : 31 * 8], r_send)


def local(interaction, cluster_moduli, cluster_fraction, plastic_flag, micro_id, macro_strain, cluster_state):
    vmem = pl.BlockSpec(memory_space=pltpu.VMEM)
    home, hom, res = pl.pallas_call(
        kernel,
        out_shape=(
            pltpu.VMEM((6, 64, 128), jnp.float32),
            pltpu.VMEM((6, 64), jnp.float32),
            pltpu.VMEM((3, 64), jnp.float32),
        ),
        in_specs=[pl.BlockSpec(memory_space=pl.ANY)] * 7,
        out_specs=(vmem, vmem, vmem),
        scratch_shapes=[
            pltpu.VMEM((6, 6, 128, 1024), jnp.bfloat16),
            pltpu.VMEM((3, 1, 128), jnp.float32),
            pltpu.VMEM((1, 128), jnp.float32),
            pltpu.VMEM((1, 128), jnp.int32),
            pltpu.VMEM((1, 64), jnp.int32),
            pltpu.VMEM((6, 64), jnp.float32),
            pltpu.VMEM((6, 64, 128), jnp.float32),
            pltpu.VMEM((6, 128, ROWS), jnp.float32),
            pltpu.VMEM((STAGES, 8, 6, ROWS, 128), jnp.bfloat16),
            pltpu.VMEM((CHUNKS, HOMES * MSG, 128), jnp.float32),
            pltpu.VMEM((CHUNKS, HOMES * MSG, 128), jnp.float32),
            pltpu.VMEM((CHUNKS, HOMES * MSG, 128), jnp.float32),
            pltpu.VMEM((CHUNKS, HOMES * MSG, 128), jnp.float32),
            pltpu.VMEM((CHUNKS, HOMES * MSG, 128), jnp.int16),
            pltpu.VMEM((CHUNKS, HOMES * MSG, 128), jnp.int16),
            pltpu.VMEM((CHUNKS, ROWS, 128), jnp.float32),
            pltpu.VMEM((6, ROWS, 128), jnp.float32),
            pltpu.VMEM((128, 128), jnp.float32),
            pltpu.VMEM((8, 8 * CHUNKS, 128), jnp.float32),
            pltpu.VMEM((HOMES * 8, 128), jnp.float32),
            pltpu.VMEM((HOMES * 8, 128), jnp.float32),
            pltpu.VMEM((8, 128), jnp.int32),
            pltpu.VMEM((2, 8, 128), jnp.int32),
            pltpu.SemaphoreType.DMA,
            pltpu.SemaphoreType.DMA((6,)),
            pltpu.SemaphoreType.DMA((CHUNKS,)),
            pltpu.SemaphoreType.DMA((CHUNKS,)),
            pltpu.SemaphoreType.DMA((STAGES,)),
            pltpu.SemaphoreType.DMA((STAGES, 6)),
            pltpu.SemaphoreType.DMA((CHUNKS,)),
            pltpu.SemaphoreType.DMA((CHUNKS,)),
            pltpu.SemaphoreType.DMA,
            pltpu.SemaphoreType.DMA,
            pltpu.SemaphoreType.DMA,
            pltpu.SemaphoreType.DMA,
            pltpu.SemaphoreType.DMA((2,)),
            pltpu.SemaphoreType.DMA((2,)),
        ],
        compiler_params=pltpu.CompilerParams(
            collective_id=0, has_side_effects=True, vmem_limit_bytes=56 * 2**20
        ),
    )(
        jnp.transpose(interaction[0], (0, 2, 1, 3)),
        jnp.transpose(cluster_moduli, (1, 0, 2)),
        cluster_fraction,
        plastic_flag,
        micro_id.reshape(1, -1),
        macro_strain.T,
        jnp.transpose(cluster_state, (1, 0, 2)),
    )
    return jnp.transpose(home, (1, 0, 2)), hom, res


def solution(mesh):
    placed = (
        P("macro", None, "micro", None, None),
        P("macro", None, "micro"),
        P("macro", "micro"),
        P("macro", "micro"),
        P("macro", None),
        P("macro", None),
        P("macro", None, "micro"),
    )
    return jax.shard_map(
        local,
        mesh=mesh,
        in_specs=placed,
        out_specs=(P("macro", None, "micro"), P(None, "macro"), P(None, "macro")),
        check_vma=False,
    )
```
